512 devices in a mesh: rows: 128 (over x, z, core), cent: 4 (over y).
Axes of the slice: x: 4, y: 4, z: 16, core: 2. Of those that a mesh axis runs over, the one named last changes fastest.
Arguments:
- embeddings: bfloat16 [65536, 768], P('rows')
- centroids: float32 [8192, 768], P(('rows', 'cent'))
- labels: int32 [65536], P('rows'), may hold values from 0 to 8191, as said below
- ranks: int32 [65536], P('rows'), may hold values from 0 to 1535, as said below
- owner_map: int32 [8192], replicated, may hold values from 0 to 127, as said below
Outputs:
- top_sim: float32 [65536], P(('rows', 'cent'))
- own_sim: float32 [65536], P(('rows', 'cent'))
- dup_sim: float32 [65536], P(('rows', 'cent'))
- cluster_peak: float32 [8192], P('rows')
The draws below stay inside these ranges and needn't reach their ends.
Inputs may be any that keep to these rules, and one draw needn't show every extreme that they name: owner_map[c] is the owner of cluster c; each owner owns exactly 64 clusters. With owner = owner_map[labels], the rows of one device (aligned blocks of 512 rows) name one owner at most 12 times; in every draw some owner is named exactly 12 times by the rows of every device. Within each cluster the ranks of its rows are 0 to its size minus one, each once; a cluster holds at most 1536 rows, and some cluster holds exactly that many.
All inputs are finite; a program needn't handle non-finite values.
Results may differ from the reference program's by a relative error of at most 0.00051.
Values may be sent and summed in bfloat16 or wider, within the bound.
A program may use at most 64 MiB of HBM per device.

```python
import math
import jax
import jax.numpy as jnp
from jax import lax

D = 768
K = 8192
TOK_DEV = 512
TOKENS = 65536
CAP = 12
KO = 64
N_ROWS = 128


def owner_plan(key):
    n_src = TOKENS // TOK_DEV
    sigma = jax.random.permutation(jax.random.fold_in(key, 101), K).astype(jnp.int32)
    owner_map = sigma % n_src
    inverse = jnp.argsort(sigma).astype(jnp.int32)
    order = jax.random.permutation(jax.random.fold_in(key, 102), n_src).astype(jnp.int32)
    hot = n_src // 8
    cold = n_src - hot
    rest = TOK_DEV - hot * CAP
    base = rest // cold
    extra = rest % cold
    shift = jax.random.randint(jax.random.fold_in(key, 103), (n_src,), 0, cold)
    position = jnp.arange(n_src, dtype=jnp.int32)
    cold_count = base + ((position[None, :] - hot + shift[:, None]) % cold < extra).astype(jnp.int32)
    counts = jnp.where(position[None, :] < hot, CAP, cold_count)
    ends = jnp.cumsum(counts, axis=1)
    slots = jnp.arange(TOK_DEV, dtype=jnp.int32)
    which = jnp.sum((ends[:, None, :] <= slots[None, :, None]).astype(jnp.int32), axis=2)
    owners = order[which]
    row_keys = jax.random.split(jax.random.fold_in(key, 104), n_src)
    shuffled = jax.vmap(lambda k, row: jax.random.permutation(k, row))(row_keys, owners)
    sub = jax.random.randint(jax.random.fold_in(key, 105), (n_src, TOK_DEV), 0, K // n_src)
    sub = jnp.where(shuffled == order[0], 0, sub)
    labels = inverse[shuffled + n_src * sub].reshape(TOKENS).astype(jnp.int32)
    return (owner_map.astype(jnp.int32), labels)


def base_directions(key):
    return jax.random.normal(jax.random.fold_in(key, 201), (K, D), jnp.float32)


def draw_owner_map(key, part):
    owner_map, labels = owner_plan(key)
    return owner_map


def draw_labels(key, part):
    owner_map, labels = owner_plan(key)
    return labels


def draw_ranks(key, part):
    owner_map, labels = owner_plan(key)
    key = jax.random.fold_in(key, 5)
    prio = jax.random.permutation(key, TOKENS).astype(jnp.int32)
    order = jnp.argsort(labels * TOKENS + prio).astype(jnp.int32)
    sorted_lab = labels[order]
    first = jnp.searchsorted(sorted_lab, sorted_lab, side='left').astype(jnp.int32)
    rank_sorted = jnp.arange(TOKENS, dtype=jnp.int32) - first
    return jnp.zeros((TOKENS,), jnp.int32).at[order].set(rank_sorted)


def draw_centroids(key, part):
    directions = base_directions(key)
    key = jax.random.fold_in(key, 3)
    spread = jax.random.uniform(key, (K, 1), jnp.float32, jnp.log(0.5), jnp.log(4.0))
    return directions * jnp.exp(spread)


def draw_embeddings(key, part):
    directions = base_directions(key)
    owner_map, labels = owner_plan(key)
    key = jax.random.fold_in(key, 4)
    scale_key, noise_key = jax.random.split(key)
    strength = jnp.exp(jax.random.uniform(scale_key, (TOKENS, 1), jnp.float32, jnp.log(0.1), jnp.log(2.0)))
    noise = jax.random.normal(noise_key, (TOKENS, D), jnp.float32)
    return (directions[labels] * strength + noise).astype(jnp.bfloat16)


def setup_inputs(seed: int = 0) -> dict:
    seeds = jax.random.split(jax.random.key(seed), 6)
    embeddings = draw_embeddings(jax.random.fold_in(seeds[5], 71), 0)
    centroids = draw_centroids(jax.random.fold_in(seeds[5], 71), 0)
    labels = draw_labels(jax.random.fold_in(seeds[5], 71), 0)
    ranks = draw_ranks(jax.random.fold_in(seeds[5], 71), 0)
    owner_map = draw_owner_map(jax.random.fold_in(seeds[5], 71), 0)
    return {"embeddings": embeddings, "centroids": centroids, "labels": labels, "ranks": ranks, "owner_map": owner_map}


def unit_rows(values):
    wide = values.astype(jnp.float32)
    scale = lax.rsqrt(lax.optimization_barrier(jnp.sum(wide * wide, axis=-1, keepdims=True)) + 1e-06)
    return (wide * scale).astype(jnp.bfloat16)

def reference(embeddings, centroids, labels, ranks, owner_map):
    unit = unit_rows(embeddings)
    cunit = unit_rows(centroids)
    block = math.gcd(TOKENS, 2048)
    column_ids = jnp.arange(K, dtype=jnp.int32)

    def score(args):
        rows_block, label_block = args
        sims = jnp.dot(rows_block, cunit.T, preferred_element_type=jnp.float32)
        best = lax.optimization_barrier(jnp.max(sims, axis=1))
        own = lax.optimization_barrier(jnp.max(jnp.where(label_block[:, None] == column_ids[None, :], sims, -4.0), axis=1))
        return (best, own)
    top_sim, own_sim = lax.map(score, (unit.reshape(TOKENS // block, block, D), labels.reshape(TOKENS // block, block)))
    top_sim = top_sim.reshape(TOKENS)
    own_sim = own_sim.reshape(TOKENS)
    sort_key = labels * TOKENS + ranks
    order = jnp.argsort(sort_key).astype(jnp.int32)
    sorted_unit = unit[order]
    sorted_lab = labels[order]
    sorted_rank = ranks[order]
    window = 3 * TOK_DEV
    padded_unit = jnp.concatenate([jnp.zeros((window, D), jnp.bfloat16), sorted_unit], axis=0)
    padded_lab = jnp.concatenate([jnp.full((window,), -1, jnp.int32), sorted_lab], axis=0)
    padded_rank = jnp.concatenate([jnp.zeros((window,), jnp.int32), sorted_rank], axis=0)
    qblock = 512

    def earlier(index):
        start = (index * qblock).astype(jnp.int32)
        query = lax.dynamic_slice_in_dim(sorted_unit, start, qblock, 0)
        qlab = lax.dynamic_slice_in_dim(sorted_lab, start, qblock, 0)
        qrank = lax.dynamic_slice_in_dim(sorted_rank, start, qblock, 0)
        keys = lax.dynamic_slice_in_dim(padded_unit, start, window + qblock, 0)
        klab = lax.dynamic_slice_in_dim(padded_lab, start, window + qblock, 0)
        krank = lax.dynamic_slice_in_dim(padded_rank, start, window + qblock, 0)
        gram = jnp.dot(query, keys.T, preferred_element_type=jnp.float32)
        keep = (qlab[:, None] == klab[None, :]) & (krank[None, :] < qrank[:, None])
        return lax.optimization_barrier(jnp.max(jnp.where(keep, gram, -1.0), axis=1))
    sorted_dup = lax.map(earlier, jnp.arange(TOKENS // qblock, dtype=jnp.int32)).reshape(TOKENS)
    dup_sim = jnp.zeros((TOKENS,), jnp.float32).at[order].set(sorted_dup)
    peak = jnp.full((K,), -1.0, jnp.float32).at[labels].max(dup_sim)
    owned = (owner_map[:, None] == jnp.arange(N_ROWS, dtype=jnp.int32)[None, :]).astype(jnp.int32)
    before = jnp.cumsum(owned, axis=0) - owned
    place = lax.optimization_barrier(jnp.sum(before * owned, axis=1)).astype(jnp.int32)
    target = owner_map * KO + place
    cluster_peak = jnp.zeros((K,), jnp.float32).at[target].set(peak)
    return (top_sim, own_sim, dup_sim, cluster_peak)
```

```python
import functools

import jax
import jax.numpy as jnp
from jax import lax
from jax.experimental import pallas as pl
from jax.experimental.pallas import tpu as pltpu
from jax.sharding import PartitionSpec as P

MESH = pl.DeviceIdType.MESH
F32 = jnp.float32
BF16 = jnp.bfloat16
I32 = jnp.int32

NX, NZ, NC, NY = 4, 16, 2, 4
CAP = 12
TOK = 512
D = 768
KB = 16
SLOTS = 32 * CAP
PIECE = 4 * CAP
RUN = 8 * CAP
KEYS = NZ * RUN
CHUNKS = 3
WIDE = D // CHUNKS
RANKS = 2048


def iota(shape, dim):
    return lax.broadcasted_iota(I32, shape, dim)


def mm(a, b, contract, precision=None):
    return lax.dot_general(
        a, b, ((contract[:1], contract[1:]), ((), ())), precision=precision, preferred_element_type=F32
    )


def exact(a, b, contract):
    return mm(a, b, contract, lax.Precision.HIGHEST)


def unit_of(wide):
    return (wide * lax.rsqrt(jnp.sum(wide * wide, axis=-1, keepdims=True) + 1e-06)).astype(BF16)


def lookup(table, ids):
    n = ids.shape[1]
    high = (iota((64, n), 0) == (ids >> 7)).astype(F32).astype(BF16)
    picked = mm(table.astype(F32).astype(BF16), high, (0, 0))
    return jnp.sum(jnp.where(iota((128, n), 0) == (ids & 127), picked, 0.0), axis=0, keepdims=True)


def twelfth(v):
    return (v * 10923) >> 17


def kernel(
    emb, cen, lab, rank, omap,
    top_out, own_out, dup_out, peak_out,
    unit2, lab2, cbuf, send1, recv1, send2, keys, meta_s, meta_r, meta_p, meta_k, code_col, code_row,
    bst, own, tsnd, trcv, fnd, fbuf, fall, fmat, dsnd, drcv, prow,
    bar_pair_s, bar_pair_r, a_s, a_r, s1_s, s1_r, m1_s, m1_r, s2_s, s2_r, m2_s, m2_r, t_s, t_r,
    r1_s, r1_r, r2_s, r2_r, r3_s, r3_r, p_s, p_r,
):
    r = lax.axis_index("rows")
    y = lax.axis_index("cent")
    c = r % NC
    z = (r // NC) % NZ
    x = r // (NC * NZ)
    me = x * NC + c

    def at(xx, zz, cc):
        return (xx * NZ + zz) * NC + cc

    def remote(src, dst, ssem, rsem, rows, cent):
        return pltpu.make_async_remote_copy(
            src_ref=src, dst_ref=dst, send_sem=ssem, recv_sem=rsem,
            device_id={"rows": rows, "cent": cent}, device_id_type=MESH,
        )

    def mate(d):
        q = (me + d) % 8
        return at(q // NC, z, q % NC)

    barrier = pltpu.get_barrier_semaphore()

    def hello(rows, cent):
        pl.semaphore_signal(barrier, inc=1, device_id={"rows": rows, "cent": cent}, device_id_type=MESH)

    for d in range(1, 8):
        hello(mate(d), y)
    for d in range(1, NZ):
        for cc in range(NC):
            hello(at(x, (z + d) % NZ, cc), y)
    for d in range(1, NY):
        for cc in range(NC):
            hello(at(x, z, cc), (y + d) % NY)

    w = z % 4
    g = z // 4
    cbuf[x, g, w] = unit_of(cen[...])
    half = pl.ds(pl.multiple_of(c * TOK, TOK), TOK)
    unit2[half, :] = unit_of(emb[...].astype(F32))
    lab2[c] = lab[...]
    pl.semaphore_wait(barrier, 7 + 2 * (NZ - 1) + 2 * (NY - 1))

    other = at(x, z, 1 - c)
    pair = [
        remote(unit2.at[half, :], unit2.at[half, :], bar_pair_s.at[0], bar_pair_r.at[0], other, y),
        remote(lab2.at[c], lab2.at[c], bar_pair_s.at[1], bar_pair_r.at[1], other, y),
    ]
    far = [
        remote(cbuf.at[x, g, w], cbuf.at[x, g, w], a_s.at[d - 1], a_r.at[d - 1], at(x, (z + 4 * d) % NZ, c), y)
        for d in range(1, 4)
    ]
    for copy in far + pair:
        copy.start()

    ids = lab[...]
    owner = lookup(omap[...], ids).astype(I32)
    named = iota((128, TOK), 0) == owner
    upper = (iota((TOK, TOK), 0) < iota((TOK, TOK), 1)).astype(F32).astype(BF16)
    before = mm(named.astype(F32).astype(BF16), upper, (1, 0))
    slot = jnp.sum(jnp.where(named, before, 0.0), axis=0, keepdims=True).astype(I32)
    xo, zo, co = owner >> 5, (owner >> 1) & 15, owner & 1
    place = zo >> 1
    mine = (co == y // 2) & (((xo + zo) & 1) == y % 2)
    line = xo * 8 + (place & 1) * 4 + (place >> 1)
    dest = jnp.where(mine, line * CAP + slot, -1)
    spread = (iota((SLOTS, TOK), 0) == dest).astype(F32)
    code = (ids * RANKS + rank[...] + 1).astype(F32)
    meta_s[0] = exact(code, spread, (1, 1))
    meta_r[me] = meta_s[0]
    spread16 = spread.astype(BF16)

    meta1 = [
        remote(meta_s.at[0], meta_r.at[me], m1_s.at[d - 1], m1_r.at[d - 1], mate(d), y) for d in range(1, 8)
    ]
    for copy in meta1:
        copy.start()
    first = []
    mine_in = pl.ds(pl.multiple_of(me * PIECE, 16), PIECE)
    for k in range(CHUNKS):
        cols = pl.ds(k * WIDE, WIDE)
        send1[:, cols] = mm(spread16, unit2[half, cols], (1, 0)).astype(BF16)
        for d in range(1, 8):
            q = (me + d) % 8
            first.append(
                remote(
                    send1.at[pl.ds(pl.multiple_of(q * PIECE, 16), PIECE), cols],
                    recv1.at[mine_in, cols],
                    s1_s.at[k * 7 + d - 1], s1_r.at[k * 7 + d - 1], mate(d), y,
                )
            )
            first[-1].start()
        recv1[mine_in, cols] = send1[mine_in, cols]

    for copy in far:
        copy.wait_recv()
    near = [
        remote(
            cbuf.at[x, :, w], cbuf.at[x, :, w], a_s.at[2 + d], a_r.at[2 + d], at(x, g * 4 + (w + d) % 4, c), y
        )
        for d in range(1, 4)
    ]
    for copy in near:
        copy.start()

    parity = (x + y) % 2
    core = y // 2
    active = (c == core) & ((x + z) % 2 == y % 2)
    my_line = z // 2

    def target(m):
        return 4 * m + 2 * c + parity

    def second(m, k):
        cols = pl.ds(k * WIDE, WIDE)
        return (
            send2.at[pl.ds(m * RUN, RUN), cols],
            keys.at[pl.ds(pl.multiple_of(z * RUN, 16), RUN), cols],
            s2_s.at[m * CHUNKS + k],
            s2_r.at[z * CHUNKS + k],
        )

    def second_meta(m):
        return (meta_p, meta_k.at[pl.ds(pl.multiple_of(z * 8, 8), 8), :], m2_s.at[m], m2_r.at[z])

    def push(parts, rows, cent, local):
        @pl.when(jnp.logical_not(local))
        def _():
            remote(*parts, rows, cent).start()

        @pl.when(local)
        def _():
            pltpu.make_async_copy(parts[0], parts[1], parts[3]).start()

    def pushed(parts, rows, cent, local):
        @pl.when(jnp.logical_not(local))
        def _():
            remote(*parts, rows, cent).wait_send()

    def to_self(m):
        return (target(m) == z) & (c == core)

    for copy in meta1:
        copy.wait_recv()
    for j in range(8):
        meta_p[j : j + 1, :] = meta_r[j]
    for m in range(4):
        push(second_meta(m), at(x, target(m), core), y, to_self(m))

    out_row = iota((SLOTS, SLOTS), 0)
    unit_no = twelfth(out_row)
    source_row = (unit_no & 7) * PIECE + (unit_no >> 3) * CAP + (out_row - unit_no * CAP)
    order = (source_row == iota((SLOTS, SLOTS), 1)).astype(F32).astype(BF16)
    for k in range(CHUNKS):
        cols = pl.ds(k * WIDE, WIDE)
        for d in range(1, 8):
            first[k * 7 + d - 1].wait_recv()
        send2[:, cols] = mm(order, recv1[:, cols], (1, 0)).astype(BF16)
        for m in range(4):
            push(second(m, k), at(x, target(m), core), y, to_self(m))

    for copy in near:
        copy.wait_recv()
    across = [
        remote(cbuf.at[x], cbuf.at[x], a_s.at[5 + d], a_r.at[5 + d], at((x + d) % NX, z, c), y) for d in range(1, 4)
    ]
    for copy in across:
        copy.start()

    for copy in pair:
        copy.wait_recv()
    bst[...] = jnp.full(bst.shape, -4.0, F32)
    own[...] = jnp.full(own.shape, -4.0, F32)

    def score(xx):
        row = iota((256, 1), 0)
        number = ((xx * NZ + (row >> 4)) * NC + c) * (NY * KB) + y * KB + (row & 15)

        def part(q, carry):
            rows = pl.ds(pl.multiple_of(q * 256, 256), 256)
            sims = mm(cbuf[xx].reshape(256, D), unit2[rows, :], (1, 1))
            bst[:, rows] = jnp.maximum(bst[:, rows], jnp.max(sims, axis=0, keepdims=True))
            here = lab2[q // 2, :, pl.ds(pl.multiple_of((q % 2) * 256, 256), 256)]
            found = jnp.max(jnp.where(number == here, sims, -4.0), axis=0, keepdims=True)
            own[:, rows] = jnp.maximum(own[:, rows], found)
            return carry

        lax.fori_loop(0, 4, part, 0)

    score(x)
    for d in range(1, 4):
        across[d - 1].wait_recv()
        score((x + NX - d) % NX)

    me_t = y * NC + c
    for q in range(8):
        rows = pl.ds((q % NC) * TOK + (q // NC) * 128, 128)
        tsnd[q, :, 0:128] = bst[:, rows]
        tsnd[q, :, 128:256] = own[:, rows]
    trcv[me_t] = tsnd[me_t]
    tops = []
    for d in range(1, 8):
        q = (me_t + d) % 8
        tops.append(remote(tsnd.at[q], trcv.at[me_t], t_s.at[d - 1], t_r.at[d - 1], at(x, z, q % NC), q // NC))
        tops[-1].start()

    def answer(zz):
        return (fnd.at[zz // 4], fbuf.at[my_line // 2], r1_s.at[zz], r1_r.at[my_line // 2])

    mid = my_line % 2
    is_mid = c == mid

    @pl.when(active)
    def _():
        for zz in range(NZ):
            pltpu.make_async_copy(meta_p, meta_k.at[pl.ds(zz * 8, 8), :], m2_r.at[zz]).wait()
        offset = (x * NC + my_line % 2) * PIECE + (my_line // 2) * CAP
        pick = ((iota((SLOTS, 128), 0) == iota((SLOTS, 128), 1) + offset) & (iota((SLOTS, 128), 1) < CAP)).astype(F32)
        codes = exact(meta_k[...], pick, (1, 0))
        key = iota((KEYS, 128), 0)
        group = twelfth(key)
        lane = iota((KEYS, 128), 1)
        tall = exact((group == lane).astype(F32), codes, (1, 0))
        code_col[...] = jnp.sum(jnp.where(key - group * CAP == lane, tall, 0.0), axis=1, keepdims=True)
        key = iota((128, KEYS), 1)
        group = twelfth(key)
        line_no = iota((128, KEYS), 0)
        flat = exact(codes, (group == line_no).astype(F32), (0, 0))
        code_row[...] = jnp.sum(jnp.where(key - group * CAP == line_no, flat, 0.0), axis=0, keepdims=True)

        for zz in range(NZ):
            for k in range(CHUNKS):
                cols = pl.ds(k * WIDE, WIDE)
                pltpu.make_async_copy(
                    send2.at[pl.ds(0, RUN), cols], keys.at[pl.ds(zz * RUN, RUN), cols], s2_r.at[zz * CHUNKS + k]
                ).wait()

        for q in range(4):
            cq = code_row[:, q * 384 : (q + 1) * 384]
            base = ((((cq.astype(I32) - 1) >> 11) << 11) + 1).astype(F32)
            query = keys[q * 384 : (q + 1) * 384, :]

            def block(b, best):
                rows = pl.ds(pl.multiple_of(b * 384, 384), 384)
                gram = mm(keys[rows, :], query, (1, 1))
                ck = code_col[rows, :]
                keep = (ck >= base) & (ck < cq)
                return jnp.maximum(best, jnp.max(jnp.where(keep, gram, -1.0), axis=0, keepdims=True))

            fnd[q] = lax.fori_loop(0, 4, block, jnp.full((1, 384), -1.0, F32))
        for zz in range(NZ):
            push(answer(zz), at(x, zz, mid), y, (zz == z) & is_mid)

        held = (omap[...] == r).astype(F32)
        held16 = held.astype(BF16)
        lower = (iota((64, 64), 1) < iota((64, 64), 0)).astype(F32).astype(BF16)
        ahead = (iota((128, 128), 0) < iota((128, 128), 1)).astype(F32).astype(BF16)
        spot = mm(held16, ahead, (1, 0)) + jnp.sum(mm(lower, held16, (1, 0)), axis=1, keepdims=True)
        spot = jnp.where(held > 0.0, spot, 0.0)
        peaks = jnp.full((64, 1), -1.0, F32)
        for q in range(4):
            ids_q = (code_row[:, q * 384 : (q + 1) * 384].astype(I32) - 1) >> 11
            spots = lookup(spot, ids_q).astype(I32)
            hit = jnp.where(iota((64, 384), 0) == spots, fnd[q], -1.0)
            peaks = jnp.maximum(peaks, jnp.max(hit, axis=1, keepdims=True))
        prow[0] = jnp.max(jnp.where(iota((64, 128), 0) == iota((64, 128), 1), peaks, -2.0), axis=0, keepdims=True)
        for d in range(1, NY):
            remote(prow.at[0], prow.at[0], p_s.at[d - 1], p_r.at[0], r, (y + d) % NY).start()

    for m in range(4):
        pltpu.make_async_copy(fnd.at[0], fbuf.at[m], r1_r.at[m]).wait()
    backs = [remote(fbuf, fall.at[me], r2_s.at[d - 1], r2_r.at[d - 1], mate(d), y) for d in range(1, 8)]
    for copy in backs:
        copy.start()
    fall[me] = fbuf[...]

    for copy in tops:
        copy.wait_recv()
    both = jnp.max(trcv[...], axis=0)
    top_out[...] = both[:, 0:128]
    own_out[...] = both[:, 128:256]

    for copy in backs:
        copy.wait_recv()
    for j in range(8):
        for m in range(4):
            fmat[j * 4 + m : j * 4 + m + 1, :] = fall[j, m]
    picked = exact(fmat[...], (iota((32, TOK), 0) == line).astype(F32), (0, 0))
    inner = (z % 4) * RUN + me * CAP + slot
    value = jnp.sum(jnp.where(iota((384, TOK), 0) == inner, picked, 0.0), axis=0, keepdims=True)
    value = jnp.where(mine, value, -2.0)
    for q in range(NY):
        dsnd[q] = value[:, q * 128 : (q + 1) * 128]
    drcv[y] = dsnd[y]
    dups = []
    for d in range(1, NY):
        q = (y + d) % NY
        dups.append(remote(dsnd.at[q], drcv.at[y], r3_s.at[d - 1], r3_r.at[d - 1], r, q))
        dups[-1].start()

    @pl.when(jnp.logical_not(active_plane(x, z, c, y)))
    def _():
        pltpu.make_async_copy(dsnd.at[0], prow.at[0], p_r.at[0]).wait()

    peak_out[...] = prow[0, :, 0:64]
    for copy in dups:
        copy.wait_recv()
    dup_out[...] = jnp.max(drcv[...], axis=0)

    for copy in pair + far + near + across + meta1 + first + tops + backs + dups:
        copy.wait_send()
    for m in range(4):
        pushed(second_meta(m), at(x, target(m), core), y, to_self(m))
        for k in range(CHUNKS):
            pushed(second(m, k), at(x, target(m), core), y, to_self(m))

    @pl.when(active)
    def _():
        for zz in range(NZ):
            pushed(answer(zz), at(x, zz, mid), y, (zz == z) & is_mid)
        for d in range(1, NY):
            remote(prow.at[0], prow.at[0], p_s.at[d - 1], p_r.at[0], r, (y + d) % NY).wait_send()


def active_plane(x, z, c, y):
    return (c == y // 2) & ((x + z) % 2 == y % 2)


def per_device(embeddings, centroids, labels, ranks, owner_map):
    dma = pltpu.SemaphoreType.DMA
    vmem = pltpu.VMEM
    row = jax.ShapeDtypeStruct((1, 128), F32)
    spec = pl.BlockSpec(memory_space=pltpu.VMEM)
    outs = pl.pallas_call(
        kernel,
        out_shape=(row, row, row, jax.ShapeDtypeStruct((1, 64), F32)),
        in_specs=[spec] * 5,
        out_specs=(spec,) * 4,
        scratch_shapes=[
            vmem((2 * TOK, D), BF16),
            vmem((2, 1, TOK), I32),
            vmem((NX, 4, 4, KB, D), BF16),
            vmem((SLOTS, D), BF16),
            vmem((SLOTS, D), BF16),
            vmem((SLOTS, D), BF16),
            vmem((KEYS, D), BF16),
            vmem((1, 1, SLOTS), F32),
            vmem((8, 1, SLOTS), F32),
            vmem((8, SLOTS), F32),
            vmem((NZ * 8, SLOTS), F32),
            vmem((KEYS, 1), F32),
            vmem((1, KEYS), F32),
            vmem((1, 2 * TOK), F32),
            vmem((1, 2 * TOK), F32),
            vmem((8, 1, 256), F32),
            vmem((8, 1, 256), F32),
            vmem((4, 1, 384), F32),
            vmem((4, 1, 384), F32),
            vmem((8, 4, 1, 384), F32),
            vmem((32, 384), F32),
            vmem((NY, 1, 128), F32),
            vmem((NY, 1, 128), F32),
            vmem((1, 1, 128), F32),
            dma((2,)), dma((2,)),
            dma((9,)), dma((9,)),
            dma((7 * CHUNKS,)), dma((7 * CHUNKS,)),
            dma((7,)), dma((7,)),
            dma((4 * CHUNKS,)), dma((NZ * CHUNKS,)),
            dma((4,)), dma((NZ,)),
            dma((7,)), dma((7,)),
            dma((NZ,)), dma((4,)),
            dma((7,)), dma((7,)),
            dma((3,)), dma((3,)),
            dma((3,)), dma((1,)),
        ],
        compiler_params=pltpu.CompilerParams(
            collective_id=0, has_side_effects=True, vmem_limit_bytes=48 * 1024 * 1024
        ),
    )(
        embeddings, centroids, labels.reshape(1, TOK), ranks.reshape(1, TOK), owner_map.reshape(64, 128)
    )
    return tuple(o.reshape(-1) for o in outs)


def solution(mesh):
    placed = (P("rows", None), P(("rows", "cent"), None), P("rows"), P("rows"), P())
    return jax.shard_map(
        per_device,
        mesh=mesh,
        in_specs=placed,
        out_specs=(P(("rows", "cent")), P(("rows", "cent")), P(("rows", "cent")), P("rows")),
        check_vma=False,
    )
```

```python
import functools

import jax
import jax.numpy as jnp
from jax import lax
from jax.experimental import pallas as pl
from jax.experimental.pallas import tpu as pltpu
from jax.sharding import PartitionSpec as P

MESH = pl.DeviceIdType.MESH
F32 = jnp.float32
BF16 = jnp.bfloat16
I32 = jnp.int32

NX, NZ, NC, NY = 4, 16, 2, 4
CAP = 12
TOK = 512
D = 768
KB = 16
SLOTS = 32 * CAP
PIECE = 4 * CAP
RUN = 8 * CAP
KEYS = NZ * RUN
STEPS = [0] + [d for k in range(1, 8) for d in (k, NZ - k)] + [8]
RANKS = 2048


def iota(shape, dim):
    return lax.broadcasted_iota(I32, shape, dim)


def mm(a, b, contract, precision=None):
    return lax.dot_general(
        a, b, ((contract[:1], contract[1:]), ((), ())), precision=precision, preferred_element_type=F32
    )


def exact(a, b, contract):
    return mm(a, b, contract, lax.Precision.HIGHEST)


def unit_of(wide):
    return (wide * lax.rsqrt(jnp.sum(wide * wide, axis=-1, keepdims=True) + 1e-06)).astype(BF16)


def lookup(table, ids):
    n = ids.shape[1]
    high = (iota((64, n), 0) == (ids >> 7)).astype(F32).astype(BF16)
    picked = mm(table.astype(F32).astype(BF16), high, (0, 0))
    return jnp.sum(jnp.where(iota((128, n), 0) == (ids & 127), picked, 0.0), axis=0, keepdims=True)


def twelfth(v):
    return (v * 10923) >> 17


def nearness(dz):
    return jnp.where(dz <= 8, jnp.maximum(2 * dz - 1, 0), 2 * (NZ - dz))


def kernel(
    emb_in, cen_in, lab_in, rank_in, omap_in,
    top_out, own_out, dup_out, peak_out,
    emb, cen, lab, rank, omap,
    unit2, lab2, cbuf, send1, recv1, send2, keys, meta_s, meta_r, meta_p, meta_k, code_col, code_row, spot_row,
    bst, own, tsnd, trcv, fnd, fbuf, fpack, fall, wanted, prow,
    in_s, pair_s, pair_r, a_s, a_r, s1_s, s1_r, m1_s, m1_r, s2_s, s2_r, m2_s, m2_r, t_s, t_r,
    r1_s, r1_r, r2_s, r2_r, p_s, p_r,
):
    r = lax.axis_index("rows")
    y = lax.axis_index("cent")
    c = r % NC
    z = (r // NC) % NZ
    x = r // (NC * NZ)
    me = x * NC + c

    def at(xx, zz, cc):
        return (xx * NZ + zz) * NC + cc

    def remote(src, dst, ssem, rsem, rows, cent):
        return pltpu.make_async_remote_copy(
            src_ref=src, dst_ref=dst, send_sem=ssem, recv_sem=rsem,
            device_id={"rows": rows, "cent": cent}, device_id_type=MESH,
        )

    def mate(d):
        q = (me + d) % 8
        return at(q // NC, z, q % NC)

    barrier = pltpu.get_barrier_semaphore()

    def hello(rows, cent):
        pl.semaphore_signal(barrier, inc=1, device_id={"rows": rows, "cent": cent}, device_id_type=MESH)

    mi = y * 8 + me

    def slice_mate(d):
        q = (mi + d) % 32
        return at((q % 8) // NC, z, q % NC), q // 8

    for d in range(1, 32):
        hello(*slice_mate(d))
    for d in range(1, NZ):
        for cc in range(NC):
            hello(at(x, (z + d) % NZ, cc), y)

    loads = [
        pltpu.make_async_copy(src, dst, in_s.at[k])
        for k, (src, dst) in enumerate(
            ((cen_in, cen), (lab_in, lab), (rank_in, rank), (omap_in, omap), (emb_in, emb))
        )
    ]
    for copy in loads:
        copy.start()
    loads[0].wait()

    w = z % 4
    g = z // 4
    cbuf[x, g, w] = unit_of(cen[...])
    pl.semaphore_wait(barrier, 31 + 2 * (NZ - 1))

    far = [
        remote(cbuf.at[x, g, w], cbuf.at[x, g, w], a_s.at[d - 1], a_r.at[d - 1], at(x, (z + 4 * d) % NZ, c), y)
        for d in range(1, 4)
    ]
    for copy in far:
        copy.start()

    for copy in loads[1:]:
        copy.wait()
    half = pl.ds(pl.multiple_of(c * TOK, TOK), TOK)
    unit2[half, :] = unit_of(emb[...].astype(F32))
    lab2[c] = lab[...]
    ids = lab[...]
    owner = lookup(omap[...], ids).astype(I32)
    named = iota((128, TOK), 0) == owner
    upper = (iota((TOK, TOK), 0) < iota((TOK, TOK), 1)).astype(F32).astype(BF16)
    before = mm(named.astype(F32).astype(BF16), upper, (1, 0))
    slot = jnp.sum(jnp.where(named, before, 0.0), axis=0, keepdims=True).astype(I32)
    xo, zo, co = owner >> 5, (owner >> 1) & 15, owner & 1
    place = zo >> 1
    mine = (co == y // 2) & (((xo + zo) & 1) == y % 2)
    line = xo * 8 + (place & 1) * 4 + (place >> 1)
    dest = jnp.where(mine, line * CAP + slot, -1)
    spread = (iota((SLOTS, TOK), 0) == dest).astype(F32)
    code = (ids * RANKS + rank[...] + 1).astype(F32)
    meta_s[0] = exact(code, spread, (1, 1))
    meta_r[me] = meta_s[0]
    send1[...] = mm(spread.astype(BF16), unit2[half, :], (1, 0)).astype(BF16)
    mine_in = pl.ds(pl.multiple_of(me * PIECE, 16), PIECE)
    recv1[mine_in, :] = send1[mine_in, :]
    plane = 2 * co + ((xo + zo) & 1)
    run_row = plane * 64 + (line >> 2) * 8 + (line & 3)
    inner = (nearness((z - zo) & 15) & 3) * RUN + me * CAP + slot
    for q in range(NY):
        lanes = slice(q * 128, (q + 1) * 128)
        wanted[q, :, 0:128] = run_row[:, lanes]
        wanted[q, :, 128:256] = inner[:, lanes]

    other = at(x, z, 1 - c)
    pair = [
        remote(unit2.at[half, :], unit2.at[half, :], pair_s.at[0], pair_r.at[0], other, y),
        remote(lab2.at[c], lab2.at[c], pair_s.at[1], pair_r.at[1], other, y),
    ]
    for copy in far:
        copy.wait_recv()
    near = [
        remote(
            cbuf.at[x, :, w], cbuf.at[x, :, w], a_s.at[2 + d], a_r.at[2 + d], at(x, (z + dz) % NZ, c), y
        )
        for d, dz in ((1, 1), (2, NZ - 1), (3, NZ - 2))
    ]
    for copy in near:
        copy.start()

    meta1 = [
        remote(meta_s.at[0], meta_r.at[me], m1_s.at[d - 1], m1_r.at[d - 1], mate(d), y) for d in range(1, 8)
    ]
    first = [
        remote(
            send1.at[pl.ds(pl.multiple_of(((me + d) % 8) * PIECE, 16), PIECE), :], recv1.at[mine_in, :],
            s1_s.at[d - 1], s1_r.at[d - 1], mate(d), y,
        )
        for d in range(1, 8)
    ]
    for copy in first + meta1 + pair:
        copy.start()

    parity = (x + y) % 2
    core = y // 2
    active = (c == core) & ((x + z) % 2 == y % 2)
    my_line = z // 2

    def target(m):
        return 4 * m + 2 * c + parity

    def spot_at(m):
        return nearness((z - target(m)) & 15)

    def second(m):
        place = spot_at(m)
        return (
            send2.at[pl.ds(m * RUN, RUN), :],
            keys.at[pl.ds(pl.multiple_of(place * RUN, 16), RUN), :],
            s2_s.at[m],
            s2_r.at[place],
        )

    def second_meta(m):
        place = spot_at(m)
        return (meta_p, meta_k.at[pl.ds(pl.multiple_of(place * 8, 8), 8), :], m2_s.at[m], m2_r.at[place])

    def push(parts, rows, cent, local):
        if local is False:
            remote(*parts, rows, cent).start()
            return

        @pl.when(jnp.logical_not(local))
        def _():
            remote(*parts, rows, cent).start()

        @pl.when(local)
        def _():
            pltpu.make_async_copy(parts[0], parts[1], parts[3]).start()

    def pushed(parts, rows, cent, local):
        if local is False:
            remote(*parts, rows, cent).wait_send()
            return

        @pl.when(jnp.logical_not(local))
        def _():
            remote(*parts, rows, cent).wait_send()

    def to_self(m):
        return (target(m) == z) & (c == core)

    for copy in meta1:
        copy.wait_recv()
    for j in range(8):
        meta_p[j : j + 1, :] = meta_r[j]
    for m in range(4):
        push(second_meta(m), at(x, target(m), core), y, to_self(m))

    out_row = iota((SLOTS, SLOTS), 0)
    unit_no = twelfth(out_row)
    source_row = (unit_no & 7) * PIECE + (unit_no >> 3) * CAP + (out_row - unit_no * CAP)
    order = (source_row == iota((SLOTS, SLOTS), 1)).astype(F32).astype(BF16)
    for copy in first:
        copy.wait_recv()
    send2[...] = mm(order, recv1[...], (1, 0)).astype(BF16)
    for m in range(4):
        push(second(m), at(x, target(m), core), y, to_self(m))

    for copy in near:
        copy.wait_recv()
    across = [
        remote(cbuf.at[x], cbuf.at[x], a_s.at[5 + d], a_r.at[5 + d], at((x + d) % NX, z, c), y) for d in range(1, 4)
    ]
    for copy in across:
        copy.start()

    @pl.when(active)
    def _():
        for zz in range(NZ):
            pltpu.make_async_copy(meta_p, meta_k.at[pl.ds(zz * 8, 8), :], m2_r.at[zz]).wait()
        offset = (x * NC + my_line % 2) * PIECE + (my_line // 2) * CAP
        pick = ((iota((SLOTS, 128), 0) == iota((SLOTS, 128), 1) + offset) & (iota((SLOTS, 128), 1) < CAP)).astype(F32)
        codes = exact(meta_k[...], pick, (1, 0))
        key = iota((KEYS, 128), 0)
        group = twelfth(key)
        lane = iota((KEYS, 128), 1)
        tall = exact((group == lane).astype(F32), codes, (1, 0))
        code_col[...] = jnp.sum(jnp.where(key - group * CAP == lane, tall, 0.0), axis=1, keepdims=True)
        key = iota((128, KEYS), 1)
        group = twelfth(key)
        line_no = iota((128, KEYS), 0)
        flat = exact(codes, (group == line_no).astype(F32), (0, 0))
        code_row[...] = jnp.sum(jnp.where(key - group * CAP == line_no, flat, 0.0), axis=0, keepdims=True)

        held = (omap[...] == r).astype(F32)
        held16 = held.astype(BF16)
        lower = (iota((64, 64), 1) < iota((64, 64), 0)).astype(F32).astype(BF16)
        ahead = (iota((128, 128), 0) < iota((128, 128), 1)).astype(F32).astype(BF16)
        spot = mm(held16, ahead, (1, 0)) + jnp.sum(mm(lower, held16, (1, 0)), axis=1, keepdims=True)
        spot = jnp.where(held > 0.0, spot, 0.0)
        for q in range(4):
            lanes = slice(q * 384, (q + 1) * 384)
            spot_row[:, lanes] = lookup(spot, (code_row[:, lanes].astype(I32) - 1) >> 11)

    for copy in pair:
        copy.wait_recv()
    bst[...] = jnp.full(bst.shape, -4.0, F32)
    own[...] = jnp.full(own.shape, -4.0, F32)

    def score(xx):
        row = iota((256, 1), 0)
        number = ((xx * NZ + (row >> 4)) * NC + c) * (NY * KB) + y * KB + (row & 15)

        def part(q, carry):
            rows = pl.ds(pl.multiple_of(q * 256, 256), 256)
            sims = mm(cbuf[xx].reshape(256, D), unit2[rows, :], (1, 1))
            bst[:, rows] = jnp.maximum(bst[:, rows], jnp.max(sims, axis=0, keepdims=True))
            here = lab2[q // 2, :, pl.ds(pl.multiple_of((q % 2) * 256, 256), 256)]
            found = jnp.max(jnp.where(number == here, sims, -4.0), axis=0, keepdims=True)
            own[:, rows] = jnp.maximum(own[:, rows], found)
            return carry

        lax.fori_loop(0, 4, part, 0)

    score(x)
    for d in range(1, 4):
        across[d - 1].wait_recv()
        score((x + NX - d) % NX)

    me_t = y * NC + c
    for q in range(8):
        rows = pl.ds((q % NC) * TOK + (q // NC) * 128, 128)
        tsnd[q, :, 0:128] = bst[:, rows]
        tsnd[q, :, 128:256] = own[:, rows]
    trcv[me_t] = tsnd[me_t]
    tops = []
    for d in range(1, 8):
        q = (me_t + d) % 8
        tops.append(remote(tsnd.at[q], trcv.at[me_t], t_s.at[d - 1], t_r.at[d - 1], at(x, z, q % NC), q // NC))
        tops[-1].start()

    for copy in tops:
        copy.wait_recv()
    both = jnp.max(trcv[...], axis=0)
    top_out[...] = both[:, 0:128]
    own_out[...] = both[:, 128:256]

    def answer(p):
        return (fnd.at[p // 4], fbuf.at[my_line // 2], r1_s.at[p], r1_r.at[my_line // 2])

    mid = my_line % 2
    is_mid = c == mid

    @pl.when(active)
    def _():
        fnd[...] = jnp.full(fnd.shape, -1.0, F32)

        def update(q, b):
            lanes = pl.ds(pl.multiple_of(q * 384, 384), 384)
            rows = pl.ds(pl.multiple_of(b * 384, 384), 384)
            cq = code_row[:, lanes]
            base = ((((cq.astype(I32) - 1) >> 11) << 11) + 1).astype(F32)
            gram = mm(keys[rows, :], keys[lanes, :], (1, 1))
            ck = code_col[rows, :]
            keep = (ck >= base) & (ck < cq)
            fnd[q] = jnp.maximum(fnd[q], jnp.max(jnp.where(keep, gram, -1.0), axis=0, keepdims=True))

        for part in range(4):
            for p in range(4 * part, 4 * part + 4):
                pltpu.make_async_copy(
                    send2.at[pl.ds(0, RUN), :], keys.at[pl.ds(p * RUN, RUN), :], s2_r.at[p]
                ).wait()

            def old(b, carry, part=part):
                update(part, b)
                update(b, part)
                return carry

            update(part, part)
            if part:
                lax.fori_loop(0, part, old, 0)

        for p in range(NZ):
            push(answer(p), at(x, (z + STEPS[p]) % NZ, mid), y, is_mid if p == 0 else False)

    for m in range(4):
        pltpu.make_async_copy(fnd.at[0], fbuf.at[m], r1_r.at[m]).wait()
    for m in range(4):
        fpack[m : m + 1, :] = fbuf[m]
    fpack[4:8, :] = jnp.zeros((4, 384), F32)
    mine_back = pl.ds(pl.multiple_of(mi * 8, 8), 8)
    backs = [
        remote(fpack, fall.at[mine_back, :], r2_s.at[d - 1], r2_r.at[d - 1], *slice_mate(d)) for d in range(1, 32)
    ]
    for copy in backs:
        copy.start()
    fall[mine_back, :] = fpack[...]

    @pl.when(active)
    def _():
        peaks = jnp.full((64, 1), -1.0, F32)
        for q in range(4):
            spots = spot_row[:, q * 384 : (q + 1) * 384].astype(I32)
            hit = jnp.where(iota((64, 384), 0) == spots, fnd[q], -1.0)
            peaks = jnp.maximum(peaks, jnp.max(hit, axis=1, keepdims=True))
        prow[0] = jnp.max(jnp.where(iota((64, 128), 0) == iota((64, 128), 1), peaks, -2.0), axis=0, keepdims=True)
        for d in range(1, NY):
            remote(prow.at[0], prow.at[0], p_s.at[d - 1], p_r.at[0], r, (y + d) % NY).start()

    rows_wanted = (iota((256, 128), 0) == wanted[y, :, 0:128]).astype(F32)
    lanes_wanted = iota((384, 128), 0) == wanted[y, :, 128:256]
    for copy in backs:
        copy.wait_recv()
    picked = exact(fall[...], rows_wanted, (0, 0))
    dup_out[...] = jnp.sum(jnp.where(lanes_wanted, picked, 0.0), axis=0, keepdims=True)

    @pl.when(jnp.logical_not(active))
    def _():
        pltpu.make_async_copy(tsnd.at[0, :, 0:128], prow.at[0], p_r.at[0]).wait()

    peak_out[...] = prow[0, :, 0:64]

    for copy in pair + far + near + across + meta1 + first + tops + backs:
        copy.wait_send()
    for m in range(4):
        pushed(second_meta(m), at(x, target(m), core), y, to_self(m))
        pushed(second(m), at(x, target(m), core), y, to_self(m))

    @pl.when(active)
    def _():
        for p in range(NZ):
            pushed(answer(p), at(x, (z + STEPS[p]) % NZ, mid), y, is_mid if p == 0 else False)
        for d in range(1, NY):
            remote(prow.at[0], prow.at[0], p_s.at[d - 1], p_r.at[0], r, (y + d) % NY).wait_send()


def per_device(embeddings, centroids, labels, ranks, owner_map):
    dma = pltpu.SemaphoreType.DMA
    vmem = pltpu.VMEM
    row = jax.ShapeDtypeStruct((1, 128), F32)
    spec = pl.BlockSpec(memory_space=pltpu.VMEM)
    outs = pl.pallas_call(
        kernel,
        out_shape=(row, row, row, jax.ShapeDtypeStruct((1, 64), F32)),
        in_specs=[pl.BlockSpec(memory_space=pl.ANY)] * 5,
        out_specs=(spec,) * 4,
        scratch_shapes=[
            vmem((TOK, D), BF16),
            vmem((KB, D), F32),
            vmem((1, TOK), I32),
            vmem((1, TOK), I32),
            vmem((64, 128), I32),
            vmem((2 * TOK, D), BF16),
            vmem((2, 1, TOK), I32),
            vmem((NX, 4, 4, KB, D), BF16),
            vmem((SLOTS, D), BF16),
            vmem((SLOTS, D), BF16),
            vmem((SLOTS, D), BF16),
            vmem((KEYS, D), BF16),
            vmem((1, 1, SLOTS), F32),
            vmem((8, 1, SLOTS), F32),
            vmem((8, SLOTS), F32),
            vmem((NZ * 8, SLOTS), F32),
            vmem((KEYS, 1), F32),
            vmem((1, KEYS), F32),
            vmem((1, KEYS), F32),
            vmem((1, 2 * TOK), F32),
            vmem((1, 2 * TOK), F32),
            vmem((8, 1, 256), F32),
            vmem((8, 1, 256), F32),
            vmem((4, 1, 384), F32),
            vmem((4, 1, 384), F32),
            vmem((8, 384), F32),
            vmem((256, 384), F32),
            vmem((NY, 1, 256), I32),
            vmem((1, 1, 128), F32),
            dma((5,)),
            dma((2,)), dma((2,)),
            dma((9,)), dma((9,)),
            dma((7,)), dma((7,)),
            dma((7,)), dma((7,)),
            dma((4,)), dma((NZ,)),
            dma((4,)), dma((NZ,)),
            dma((7,)), dma((7,)),
            dma((NZ,)), dma((4,)),
            dma((31,)), dma((31,)),
            dma((3,)), dma((1,)),
        ],
        compiler_params=pltpu.CompilerParams(
            collective_id=0, has_side_effects=True, vmem_limit_bytes=62 * 1024 * 1024
        ),
    )(
        embeddings, centroids, labels.reshape(1, TOK), ranks.reshape(1, TOK), owner_map.reshape(64, 128)
    )
    return tuple(o.reshape(-1) for o in outs)


def solution(mesh):
    placed = (P("rows", None), P(("rows", "cent"), None), P("rows"), P("rows"), P())
    return jax.shard_map(
        per_device,
        mesh=mesh,
        in_specs=placed,
        out_specs=(P(("rows", "cent")), P(("rows", "cent")), P(("rows", "cent")), P("rows")),
        check_vma=False,
    )
```

```python
import functools

import jax
import jax.numpy as jnp
from jax import lax
from jax.experimental import pallas as pl
from jax.experimental.pallas import tpu as pltpu
from jax.sharding import PartitionSpec as P

MESH = pl.DeviceIdType.MESH
F32 = jnp.float32
BF16 = jnp.bfloat16
I32 = jnp.int32

NX, NZ, NC, NY = 4, 16, 2, 4
CAP = 12
TOK = 512
D = 768
KB = 16
SLOTS = 32 * CAP
PIECE = 4 * CAP
RUN = 8 * CAP
KEYS = NZ * RUN
STEPS = [0] + [d for k in range(1, 8) for d in (k, NZ - k)] + [8]
RANKS = 2048


def iota(shape, dim):
    return lax.broadcasted_iota(I32, shape, dim)


def mm(a, b, contract, precision=None):
    return lax.dot_general(
        a, b, ((contract[:1], contract[1:]), ((), ())), precision=precision, preferred_element_type=F32
    )


def exact(a, b, contract):
    return mm(a, b, contract, lax.Precision.HIGHEST)


def unit_of(wide):
    return (wide * lax.rsqrt(jnp.sum(wide * wide, axis=-1, keepdims=True) + 1e-06)).astype(BF16)


def lookup(table, ids):
    n = ids.shape[1]
    high = (iota((64, n), 0) == (ids >> 7)).astype(F32).astype(BF16)
    picked = mm(table.astype(F32).astype(BF16), high, (0, 0))
    return jnp.sum(jnp.where(iota((128, n), 0) == (ids & 127), picked, 0.0), axis=0, keepdims=True)


def twelfth(v):
    return (v * 10923) >> 17


def nearness(dz):
    return jnp.where(dz <= 8, jnp.maximum(2 * dz - 1, 0), 2 * (NZ - dz))


def kernel(
    emb_in, cen_in, lab_in, rank_in, omap_in,
    top_out, own_out, dup_out, peak_out,
    emb, cen, lab, rank, omap,
    unit2, lab2, cbuf, send1, recv1, send2, keys, meta_s, meta_r, meta_p, meta_k, code_col, code_row, base_col, base_row, spot_row,
    bst, own, tsnd, trcv, fnd, best_col, runs, fbuf, fpack, fall, wanted, prow,
    in_s, pair_s, pair_r, a_s, a_r, s1_s, s1_r, m1_s, m1_r, s2_s, s2_r, m2_s, m2_r, t_s, t_r,
    r1_s, r1_r, r2_s, r2_r, p_s, p_r,
):
    r = lax.axis_index("rows")
    y = lax.axis_index("cent")
    c = r % NC
    z = (r // NC) % NZ
    x = r // (NC * NZ)
    me = x * NC + c

    def at(xx, zz, cc):
        return (xx * NZ + zz) * NC + cc

    def remote(src, dst, ssem, rsem, rows, cent):
        return pltpu.make_async_remote_copy(
            src_ref=src, dst_ref=dst, send_sem=ssem, recv_sem=rsem,
            device_id={"rows": rows, "cent": cent}, device_id_type=MESH,
        )

    def mate(d):
        q = (me + d) % 8
        return at(q // NC, z, q % NC)

    barrier = pltpu.get_barrier_semaphore()
    runs[...] = jnp.zeros(runs.shape, F32)
    fpack[...] = jnp.zeros(fpack.shape, F32)

    def hello(rows, cent):
        pl.semaphore_signal(barrier, inc=1, device_id={"rows": rows, "cent": cent}, device_id_type=MESH)

    mi = y * 8 + me

    def slice_mate(d):
        q = (mi + d) % 32
        return at((q % 8) // NC, z, q % NC), q // 8

    for d in range(1, 32):
        hello(*slice_mate(d))
    for d in range(1, NZ):
        for cc in range(NC):
            hello(at(x, (z + d) % NZ, cc), y)

    loads = [
        pltpu.make_async_copy(src, dst, in_s.at[k])
        for k, (src, dst) in enumerate(
            ((cen_in, cen), (lab_in, lab), (rank_in, rank), (omap_in, omap), (emb_in, emb))
        )
    ]
    for copy in loads:
        copy.start()
    for copy in loads:
        copy.wait()

    w = z % 4
    g = z // 4
    cbuf[x, g, w] = unit_of(cen[...])
    half = pl.ds(pl.multiple_of(c * TOK, TOK), TOK)
    unit2[half, :] = unit_of(emb[...].astype(F32))
    lab2[c] = lab[...]
    ids = lab[...]
    owner = lookup(omap[...], ids).astype(I32)
    named = iota((128, TOK), 0) == owner
    upper = (iota((TOK, TOK), 0) < iota((TOK, TOK), 1)).astype(F32).astype(BF16)
    before = mm(named.astype(F32).astype(BF16), upper, (1, 0))
    slot = jnp.sum(jnp.where(named, before, 0.0), axis=0, keepdims=True).astype(I32)
    xo, zo, co = owner >> 5, (owner >> 1) & 15, owner & 1
    place = zo >> 1
    mine = (co == y // 2) & (((xo + zo) & 1) == y % 2)
    line = xo * 8 + (place & 1) * 4 + (place >> 1)
    dest = jnp.where(mine, line * CAP + slot, -1)
    spread = (iota((SLOTS, TOK), 0) == dest).astype(F32)
    code = (ids * RANKS + rank[...] + 1).astype(F32)
    meta_s[0] = exact(code, spread, (1, 1))
    meta_r[me] = meta_s[0]
    send1[...] = mm(spread.astype(BF16), unit2[half, :], (1, 0)).astype(BF16)
    mine_in = pl.ds(pl.multiple_of(me * PIECE, 16), PIECE)
    recv1[mine_in, :] = send1[mine_in, :]
    plane = 2 * co + ((xo + zo) & 1)
    run_row = plane * 64 + (line >> 2) * 8 + (line & 3)
    inner = me * CAP + slot
    for q in range(NY):
        lanes = slice(q * 128, (q + 1) * 128)
        wanted[q, :, 0:128] = run_row[:, lanes]
        wanted[q, :, 128:256] = inner[:, lanes]

    pl.semaphore_wait(barrier, 31 + 2 * (NZ - 1))

    far = [
        remote(cbuf.at[x, g, w], cbuf.at[x, g, w], a_s.at[d - 1], a_r.at[d - 1], at(x, (z + 4 * d) % NZ, c), y)
        for d in range(1, 4)
    ]
    other = at(x, z, 1 - c)
    pair = [
        remote(unit2.at[half, :], unit2.at[half, :], pair_s.at[0], pair_r.at[0], other, y),
        remote(lab2.at[c], lab2.at[c], pair_s.at[1], pair_r.at[1], other, y),
    ]
    meta1 = [
        remote(meta_s.at[0], meta_r.at[me], m1_s.at[d - 1], m1_r.at[d - 1], mate(d), y) for d in range(1, 8)
    ]
    first = [
        remote(
            send1.at[pl.ds(pl.multiple_of(((me + d) % 8) * PIECE, 16), PIECE), :], recv1.at[mine_in, :],
            s1_s.at[d - 1], s1_r.at[d - 1], mate(d), y,
        )
        for d in range(1, 8)
    ]
    for copy in first + far + meta1 + pair:
        copy.start()

    for copy in far:
        copy.wait_recv()
    near = [
        remote(
            cbuf.at[x, :, w], cbuf.at[x, :, w], a_s.at[2 + d], a_r.at[2 + d], at(x, (z + dz) % NZ, c), y
        )
        for d, dz in ((1, 1), (2, NZ - 1), (3, NZ - 2))
    ]
    for copy in near:
        copy.start()

    parity = (x + y) % 2
    core = y // 2
    active = (c == core) & ((x + z) % 2 == y % 2)
    my_line = z // 2

    def target(m):
        return 4 * m + 2 * c + parity

    def spot_at(m):
        return nearness((z - target(m)) & 15)

    def second(m):
        place = spot_at(m)
        return (
            send2.at[pl.ds(m * RUN, RUN), :],
            keys.at[pl.ds(pl.multiple_of(place * RUN, 16), RUN), :],
            s2_s.at[m],
            s2_r.at[place],
        )

    def second_meta(m):
        place = spot_at(m)
        return (meta_p, meta_k.at[pl.ds(pl.multiple_of(place * 8, 8), 8), :], m2_s.at[m], m2_r.at[place])

    def push(parts, rows, cent, local):
        if local is False:
            remote(*parts, rows, cent).start()
            return

        @pl.when(jnp.logical_not(local))
        def _():
            remote(*parts, rows, cent).start()

        @pl.when(local)
        def _():
            pltpu.make_async_copy(parts[0], parts[1], parts[3]).start()

    def pushed(parts, rows, cent, local):
        if local is False:
            remote(*parts, rows, cent).wait_send()
            return

        @pl.when(jnp.logical_not(local))
        def _():
            remote(*parts, rows, cent).wait_send()

    def to_self(m):
        return (target(m) == z) & (c == core)

    for copy in meta1:
        copy.wait_recv()
    for j in range(8):
        meta_p[j : j + 1, :] = meta_r[j]
    for m in range(4):
        push(second_meta(m), at(x, target(m), core), y, to_self(m))

    out_row = iota((SLOTS, SLOTS), 0)
    unit_no = twelfth(out_row)
    source_row = (unit_no & 7) * PIECE + (unit_no >> 3) * CAP + (out_row - unit_no * CAP)
    order = (source_row == iota((SLOTS, SLOTS), 1)).astype(F32).astype(BF16)
    for copy in first:
        copy.wait_recv()
    send2[...] = mm(order, recv1[...], (1, 0)).astype(BF16)
    for m in range(4):
        push(second(m), at(x, target(m), core), y, to_self(m))

    for copy in near:
        copy.wait_recv()
    across = [
        remote(cbuf.at[x], cbuf.at[x], a_s.at[5 + d], a_r.at[5 + d], at((x + d) % NX, z, c), y) for d in range(1, 4)
    ]
    for copy in across:
        copy.start()

    @pl.when(active)
    def _():
        for zz in range(NZ):
            pltpu.make_async_copy(meta_p, meta_k.at[pl.ds(zz * 8, 8), :], m2_r.at[zz]).wait()
        offset = (x * NC + my_line % 2) * PIECE + (my_line // 2) * CAP
        pick = ((iota((SLOTS, 128), 0) == iota((SLOTS, 128), 1) + offset) & (iota((SLOTS, 128), 1) < CAP)).astype(F32)
        codes = exact(meta_k[...], pick, (1, 0))
        key = iota((KEYS, 128), 0)
        group = twelfth(key)
        lane = iota((KEYS, 128), 1)
        tall = exact((group == lane).astype(F32), codes, (1, 0))
        code_col[...] = jnp.sum(jnp.where(key - group * CAP == lane, tall, 0.0), axis=1, keepdims=True)
        key = iota((128, KEYS), 1)
        group = twelfth(key)
        line_no = iota((128, KEYS), 0)
        flat = exact(codes, (group == line_no).astype(F32), (0, 0))
        code_row[...] = jnp.sum(jnp.where(key - group * CAP == line_no, flat, 0.0), axis=0, keepdims=True)

        def floor_of(code):
            return ((((code.astype(I32) - 1) >> 11) << 11) + 1).astype(F32)

        base_row[...] = floor_of(code_row[...])
        base_col[...] = floor_of(code_col[...])
        held = (omap[...] == r).astype(F32)
        held16 = held.astype(BF16)
        lower = (iota((64, 64), 1) < iota((64, 64), 0)).astype(F32).astype(BF16)
        ahead = (iota((128, 128), 0) < iota((128, 128), 1)).astype(F32).astype(BF16)
        spot = mm(held16, ahead, (1, 0)) + jnp.sum(mm(lower, held16, (1, 0)), axis=1, keepdims=True)
        spot = jnp.where(held > 0.0, spot, 0.0)
        for q in range(4):
            lanes = slice(q * 384, (q + 1) * 384)
            spot_row[:, lanes] = lookup(spot, (code_row[:, lanes].astype(I32) - 1) >> 11)

    def answer(p):
        return (runs.at[p], fbuf.at[my_line // 2], r1_s.at[p], r1_r.at[my_line // 2])

    mid = my_line % 2
    is_mid = c == mid

    @pl.when(active)
    def _():
        fnd[...] = jnp.full(fnd.shape, -1.0, F32)
        best_col[...] = jnp.full(best_col.shape, -1.0, F32)

        def update(q, b, both_ways):
            lanes = pl.ds(pl.multiple_of(q * 384, 384), 384)
            rows = pl.ds(pl.multiple_of(b * 384, 384), 384)
            cq, bq = code_row[:, lanes], base_row[:, lanes]
            gram = mm(keys[rows, :], keys[lanes, :], (1, 1))
            ck = code_col[rows, :]
            keep = (ck >= bq) & (ck < cq)
            fnd[q] = jnp.maximum(fnd[q], jnp.max(jnp.where(keep, gram, -1.0), axis=0, keepdims=True))
            if both_ways:
                keep = (cq >= base_col[rows, :]) & (cq < ck)
                found = jnp.max(jnp.where(keep, gram, -1.0), axis=1, keepdims=True)
                best_col[rows, :] = jnp.maximum(best_col[rows, :], found)

        for part in range(4):
            for p in range(4 * part, 4 * part + 4):
                pltpu.make_async_copy(
                    send2.at[pl.ds(0, RUN), :], keys.at[pl.ds(p * RUN, RUN), :], s2_r.at[p]
                ).wait()

            def old(b, carry, part=part):
                update(part, b, True)
                return carry

            update(part, part, False)
            if part:
                lax.fori_loop(0, part, old, 0)

        for q in range(4):
            best = fnd[q]
            if q < 3:
                diagonal = iota((128, 128), 0) == iota((128, 128), 1)
                turned = [
                    jnp.max(
                        jnp.where(diagonal, best_col[q * 384 + k * 128 : q * 384 + (k + 1) * 128, :], -2.0),
                        axis=0, keepdims=True,
                    )
                    for k in range(3)
                ]
                best = jnp.maximum(best, jnp.concatenate(turned, axis=1))
                fnd[q] = best
            for k in range(4):
                runs[q * 4 + k, :, 0:RUN] = best[:, k * RUN : (k + 1) * RUN]
        for p in reversed(range(NZ)):
            push(answer(p), at(x, (z + STEPS[p]) % NZ, mid), y, is_mid if p == 0 else False)

    for copy in pair:
        copy.wait_recv()
    bst[...] = jnp.full(bst.shape, -4.0, F32)
    own[...] = jnp.full(own.shape, -4.0, F32)

    def score(xx):
        row = iota((256, 1), 0)
        number = ((xx * NZ + (row >> 4)) * NC + c) * (NY * KB) + y * KB + (row & 15)

        def part(q, carry):
            rows = pl.ds(pl.multiple_of(q * 256, 256), 256)
            sims = mm(cbuf[xx].reshape(256, D), unit2[rows, :], (1, 1))
            bst[:, rows] = jnp.maximum(bst[:, rows], jnp.max(sims, axis=0, keepdims=True))
            here = lab2[q // 2, :, pl.ds(pl.multiple_of((q % 2) * 256, 256), 256)]
            found = jnp.max(jnp.where(number == here, sims, -4.0), axis=0, keepdims=True)
            own[:, rows] = jnp.maximum(own[:, rows], found)
            return carry

        lax.fori_loop(0, 4, part, 0)

    score(x)
    for d in range(1, 4):
        across[d - 1].wait_recv()
        score((x + NX - d) % NX)

    me_t = y * NC + c
    for q in range(8):
        rows = pl.ds((q % NC) * TOK + (q // NC) * 128, 128)
        tsnd[q, :, 0:128] = bst[:, rows]
        tsnd[q, :, 128:256] = own[:, rows]
    trcv[me_t] = tsnd[me_t]
    tops = []
    for d in range(1, 8):
        q = (me_t + d) % 8
        tops.append(remote(tsnd.at[q], trcv.at[me_t], t_s.at[d - 1], t_r.at[d - 1], at(x, z, q % NC), q // NC))
        tops[-1].start()

    for m in range(4):
        pltpu.make_async_copy(runs.at[0], fbuf.at[m], r1_r.at[m]).wait()
    for m in range(4):
        fpack[m : m + 1, :] = fbuf[m]
    mine_back = pl.ds(pl.multiple_of(mi * 8, 8), 8)
    backs = [
        remote(fpack, fall.at[mine_back, :], r2_s.at[d - 1], r2_r.at[d - 1], *slice_mate(d)) for d in range(1, 32)
    ]
    for copy in backs:
        copy.start()
    fall[mine_back, :] = fpack[...]

    @pl.when(active)
    def _():
        peaks = jnp.full((64, 1), -1.0, F32)
        for q in range(4):
            spots = spot_row[:, q * 384 : (q + 1) * 384].astype(I32)
            hit = jnp.where(iota((64, 384), 0) == spots, fnd[q], -1.0)
            peaks = jnp.maximum(peaks, jnp.max(hit, axis=1, keepdims=True))
        prow[0] = jnp.max(jnp.where(iota((64, 128), 0) == iota((64, 128), 1), peaks, -2.0), axis=0, keepdims=True)
        for d in range(1, NY):
            remote(prow.at[0], prow.at[0], p_s.at[d - 1], p_r.at[0], r, (y + d) % NY).start()

    for copy in tops:
        copy.wait_recv()
    both = jnp.max(trcv[...], axis=0)
    top_out[...] = both[:, 0:128]
    own_out[...] = both[:, 128:256]

    rows_wanted = (iota((256, 128), 0) == wanted[y, :, 0:128]).astype(F32)
    lanes_wanted = iota((128, 128), 0) == wanted[y, :, 128:256]
    for copy in backs:
        copy.wait_recv()
    picked = exact(fall[...], rows_wanted, (0, 0))
    dup_out[...] = jnp.sum(jnp.where(lanes_wanted, picked, 0.0), axis=0, keepdims=True)

    @pl.when(jnp.logical_not(active))
    def _():
        pltpu.make_async_copy(tsnd.at[0, :, 0:128], prow.at[0], p_r.at[0]).wait()

    peak_out[...] = prow[0, :, 0:64]

    for copy in pair + far + near + across + meta1 + first + tops + backs:
        copy.wait_send()
    for m in range(4):
        pushed(second_meta(m), at(x, target(m), core), y, to_self(m))
        pushed(second(m), at(x, target(m), core), y, to_self(m))

    @pl.when(active)
    def _():
        for p in range(NZ):
            pushed(answer(p), at(x, (z + STEPS[p]) % NZ, mid), y, is_mid if p == 0 else False)
        for d in range(1, NY):
            remote(prow.at[0], prow.at[0], p_s.at[d - 1], p_r.at[0], r, (y + d) % NY).wait_send()


def per_device(embeddings, centroids, labels, ranks, owner_map):
    dma = pltpu.SemaphoreType.DMA
    vmem = pltpu.VMEM
    row = jax.ShapeDtypeStruct((1, 128), F32)
    spec = pl.BlockSpec(memory_space=pltpu.VMEM)
    outs = pl.pallas_call(
        kernel,
        out_shape=(row, row, row, jax.ShapeDtypeStruct((1, 64), F32)),
        in_specs=[pl.BlockSpec(memory_space=pl.ANY)] * 5,
        out_specs=(spec,) * 4,
        scratch_shapes=[
            vmem((TOK, D), BF16),
            vmem((KB, D), F32),
            vmem((1, TOK), I32),
            vmem((1, TOK), I32),
            vmem((64, 128), I32),
            vmem((2 * TOK, D), BF16),
            vmem((2, 1, TOK), I32),
            vmem((NX, 4, 4, KB, D), BF16),
            vmem((SLOTS, D), BF16),
            vmem((SLOTS, D), BF16),
            vmem((SLOTS, D), BF16),
            vmem((KEYS, D), BF16),
            vmem((1, 1, SLOTS), F32),
            vmem((8, 1, SLOTS), F32),
            vmem((8, SLOTS), F32),
            vmem((NZ * 8, SLOTS), F32),
            vmem((KEYS, 1), F32),
            vmem((1, KEYS), F32),
            vmem((KEYS, 1), F32),
            vmem((1, KEYS), F32),
            vmem((1, KEYS), F32),
            vmem((1, 2 * TOK), F32),
            vmem((1, 2 * TOK), F32),
            vmem((8, 1, 256), F32),
            vmem((8, 1, 256), F32),
            vmem((4, 1, 384), F32),
            vmem((KEYS, 1), F32),
            vmem((NZ, 1, 128), F32),
            vmem((4, 1, 128), F32),
            vmem((8, 128), F32),
            vmem((256, 128), F32),
            vmem((NY, 1, 256), I32),
            vmem((1, 1, 128), F32),
            dma((5,)),
            dma((2,)), dma((2,)),
            dma((9,)), dma((9,)),
            dma((7,)), dma((7,)),
            dma((7,)), dma((7,)),
            dma((4,)), dma((NZ,)),
            dma((4,)), dma((NZ,)),
            dma((7,)), dma((7,)),
            dma((NZ,)), dma((4,)),
            dma((31,)), dma((31,)),
            dma((3,)), dma((1,)),
        ],
        compiler_params=pltpu.CompilerParams(
            collective_id=0, has_side_effects=True, vmem_limit_bytes=62 * 1024 * 1024
        ),
    )(
        embeddings, centroids, labels.reshape(1, TOK), ranks.reshape(1, TOK), owner_map.reshape(64, 128)
    )
    return tuple(o.reshape(-1) for o in outs)


def solution(mesh):
    placed = (P("rows", None), P(("rows", "cent"), None), P("rows"), P("rows"), P())
    return jax.shard_map(
        per_device,
        mesh=mesh,
        in_specs=placed,
        out_specs=(P(("rows", "cent")), P(("rows", "cent")), P(("rows", "cent")), P("rows")),
        check_vma=False,
    )
```

```python
import functools

import jax
import jax.numpy as jnp
from jax import lax
from jax.experimental import pallas as pl
from jax.experimental.pallas import tpu as pltpu
from jax.sharding import PartitionSpec as P

MESH = pl.DeviceIdType.MESH
F32 = jnp.float32
BF16 = jnp.bfloat16
I32 = jnp.int32

NX, NZ, NC, NY = 4, 16, 2, 4
CAP = 12
TOK = 512
D = 768
KB = 16
SLOTS = 32 * CAP
PIECE = 4 * CAP
RUN = 8 * CAP
KEYS = NZ * RUN
STEPS = [0] + [d for k in range(1, 8) for d in (k, NZ - k)] + [8]
RANKS = 2048


def iota(shape, dim):
    return lax.broadcasted_iota(I32, shape, dim)


def mm(a, b, contract, precision=None):
    return lax.dot_general(
        a, b, ((contract[:1], contract[1:]), ((), ())), precision=precision, preferred_element_type=F32
    )


def exact(a, b, contract):
    return mm(a, b, contract, lax.Precision.HIGHEST)


def unit_of(wide):
    return (wide * lax.rsqrt(jnp.sum(wide * wide, axis=-1, keepdims=True) + 1e-06)).astype(BF16)


def lookup(table, ids):
    n = ids.shape[1]
    high = (iota((64, n), 0) == (ids >> 7)).astype(F32).astype(BF16)
    picked = mm(table.astype(F32).astype(BF16), high, (0, 0))
    return jnp.sum(jnp.where(iota((128, n), 0) == (ids & 127), picked, 0.0), axis=0, keepdims=True)


def twelfth(v):
    return (v * 10923) >> 17


def nearness(dz):
    return jnp.where(dz <= 8, jnp.maximum(2 * dz - 1, 0), 2 * (NZ - dz))


def kernel(
    emb_in, cen_in, lab_in, rank_in, omap_in,
    top_out, own_out, dup_out, peak_out,
    emb, cen, lab, rank, omap,
    unit2, lab2, cbuf, send1, recv1, send2, keys, meta_s, meta_r, meta_p, meta_k, code_col, code_row, base_col, base_row, spot_row,
    bst, own, tsnd, trcv, fnd, best_col, runs, fbuf, fpack, fall, wanted, prow,
    in_s, pair_s, pair_r, a_s, a_r, s1_s, s1_r, m1_s, m1_r, s2_s, s2_r, m2_s, m2_r, t_s, t_r,
    r1_s, r1_r, r2_s, r2_r, p_s, p_r,
):
    r = lax.axis_index("rows")
    y = lax.axis_index("cent")
    c = r % NC
    z = (r // NC) % NZ
    x = r // (NC * NZ)
    me = x * NC + c

    def at(xx, zz, cc):
        return (xx * NZ + zz) * NC + cc

    def remote(src, dst, ssem, rsem, rows, cent):
        return pltpu.make_async_remote_copy(
            src_ref=src, dst_ref=dst, send_sem=ssem, recv_sem=rsem,
            device_id={"rows": rows, "cent": cent}, device_id_type=MESH,
        )

    def mate(d):
        q = (me + d) % 8
        return at(q // NC, z, q % NC)

    barrier = pltpu.get_barrier_semaphore()
    runs[...] = jnp.zeros(runs.shape, F32)
    fpack[...] = jnp.zeros(fpack.shape, F32)

    def hello(rows, cent):
        pl.semaphore_signal(barrier, inc=1, device_id={"rows": rows, "cent": cent}, device_id_type=MESH)

    mi = y * 8 + me

    def slice_mate(d):
        q = (mi + d) % 32
        return at((q % 8) // NC, z, q % NC), q // 8

    for d in range(1, 32):
        hello(*slice_mate(d))
    for d in range(1, NZ):
        for cc in range(NC):
            hello(at(x, (z + d) % NZ, cc), y)

    loads = [
        pltpu.make_async_copy(src, dst, in_s.at[k])
        for k, (src, dst) in enumerate(
            ((cen_in, cen), (lab_in, lab), (rank_in, rank), (omap_in, omap), (emb_in, emb))
        )
    ]
    for copy in loads:
        copy.start()
    for copy in loads:
        copy.wait()

    w = z % 4
    g = z // 4
    cbuf[x, g, w] = unit_of(cen[...])
    half = pl.ds(pl.multiple_of(c * TOK, TOK), TOK)
    unit2[half, :] = unit_of(emb[...].astype(F32))
    lab2[c] = lab[...]
    ids = lab[...]
    owner = lookup(omap[...], ids).astype(I32)
    named = iota((128, TOK), 0) == owner
    upper = (iota((TOK, TOK), 0) < iota((TOK, TOK), 1)).astype(F32).astype(BF16)
    before = mm(named.astype(F32).astype(BF16), upper, (1, 0))
    slot = jnp.sum(jnp.where(named, before, 0.0), axis=0, keepdims=True).astype(I32)
    xo, zo, co = owner >> 5, (owner >> 1) & 15, owner & 1
    place = zo >> 1
    mine = (co == y // 2) & (((xo + zo) & 1) == y % 2)
    line = xo * 8 + (place & 1) * 4 + (place >> 1)
    dest = jnp.where(mine, line * CAP + slot, -1)
    spread = (iota((SLOTS, TOK), 0) == dest).astype(F32)
    code = (ids * RANKS + rank[...] + 1).astype(F32)
    meta_s[0] = exact(code, spread, (1, 1))
    meta_r[me] = meta_s[0]
    send1[...] = mm(spread.astype(BF16), unit2[half, :], (1, 0)).astype(BF16)
    mine_in = pl.ds(pl.multiple_of(me * PIECE, 16), PIECE)
    recv1[mine_in, :] = send1[mine_in, :]
    plane = 2 * co + ((xo + zo) & 1)
    run_row = plane * 64 + (line >> 2) * 8 + (line & 3)
    inner = me * CAP + slot
    for q in range(NY):
        lanes = slice(q * 128, (q + 1) * 128)
        wanted[q, :, 0:128] = run_row[:, lanes]
        wanted[q, :, 128:256] = inner[:, lanes]

    pl.semaphore_wait(barrier, 31 + 2 * (NZ - 1))

    far = [
        remote(cbuf.at[x, g, w], cbuf.at[x, g, w], a_s.at[d - 1], a_r.at[d - 1], at(x, (z + 4 * d) % NZ, c), y)
        for d in range(1, 4)
    ]
    other = at(x, z, 1 - c)
    pair = [
        remote(unit2.at[half, :], unit2.at[half, :], pair_s.at[0], pair_r.at[0], other, y),
        remote(lab2.at[c], lab2.at[c], pair_s.at[1], pair_r.at[1], other, y),
    ]
    meta1 = [
        remote(meta_s.at[0], meta_r.at[me], m1_s.at[d - 1], m1_r.at[d - 1], mate(d), y) for d in range(1, 8)
    ]
    first = [
        remote(
            send1.at[pl.ds(pl.multiple_of(((me + d) % 8) * PIECE, 16), PIECE), :], recv1.at[mine_in, :],
            s1_s.at[d - 1], s1_r.at[d - 1], mate(d), y,
        )
        for d in range(1, 8)
    ]
    for copy in first + far + meta1 + pair:
        copy.start()

    for copy in far:
        copy.wait_recv()
    near = [
        remote(
            cbuf.at[x, :, w], cbuf.at[x, :, w], a_s.at[2 + d], a_r.at[2 + d], at(x, (z + dz) % NZ, c), y
        )
        for d, dz in ((1, 1), (2, NZ - 1), (3, NZ - 2))
    ]
    for copy in near:
        copy.start()

    parity = (x + y) % 2
    core = y // 2
    active = (c == core) & ((x + z) % 2 == y % 2)
    my_line = z // 2

    def target(m):
        return 4 * m + 2 * c + parity

    def spot_at(m):
        return nearness((z - target(m)) & 15)

    def second(m):
        place = spot_at(m)
        return (
            send2.at[pl.ds(m * RUN, RUN), :],
            keys.at[pl.ds(pl.multiple_of(place * RUN, 16), RUN), :],
            s2_s.at[m],
            s2_r.at[place],
        )

    def second_meta(m):
        place = spot_at(m)
        return (meta_p, meta_k.at[pl.ds(pl.multiple_of(place * 8, 8), 8), :], m2_s.at[m], m2_r.at[place])

    def push(parts, rows, cent, local):
        if local is False:
            remote(*parts, rows, cent).start()
            return

        @pl.when(jnp.logical_not(local))
        def _():
            remote(*parts, rows, cent).start()

        @pl.when(local)
        def _():
            pltpu.make_async_copy(parts[0], parts[1], parts[3]).start()

    def pushed(parts, rows, cent, local):
        if local is False:
            remote(*parts, rows, cent).wait_send()
            return

        @pl.when(jnp.logical_not(local))
        def _():
            remote(*parts, rows, cent).wait_send()

    def to_self(m):
        return (target(m) == z) & (c == core)

    for copy in meta1:
        copy.wait_recv()
    for j in range(8):
        meta_p[j : j + 1, :] = meta_r[j]
    for m in range(4):
        push(second_meta(m), at(x, target(m), core), y, to_self(m))

    out_row = iota((SLOTS, SLOTS), 0)
    unit_no = twelfth(out_row)
    source_row = (unit_no & 7) * PIECE + (unit_no >> 3) * CAP + (out_row - unit_no * CAP)
    order = (source_row == iota((SLOTS, SLOTS), 1)).astype(F32).astype(BF16)
    for copy in first:
        copy.wait_recv()
    send2[...] = mm(order, recv1[...], (1, 0)).astype(BF16)
    for m in range(4):
        push(second(m), at(x, target(m), core), y, to_self(m))

    for copy in near:
        copy.wait_recv()
    across = [
        remote(cbuf.at[x], cbuf.at[x], a_s.at[5 + d], a_r.at[5 + d], at((x + d) % NX, z, c), y) for d in range(1, 4)
    ]
    for copy in across:
        copy.start()

    @pl.when(active)
    def _():
        for zz in range(NZ):
            pltpu.make_async_copy(meta_p, meta_k.at[pl.ds(zz * 8, 8), :], m2_r.at[zz]).wait()
        offset = (x * NC + my_line % 2) * PIECE + (my_line // 2) * CAP
        pick = ((iota((SLOTS, 128), 0) == iota((SLOTS, 128), 1) + offset) & (iota((SLOTS, 128), 1) < CAP)).astype(F32)
        codes = exact(meta_k[...], pick, (1, 0))
        key = iota((KEYS, 128), 0)
        group = twelfth(key)
        lane = iota((KEYS, 128), 1)
        tall = exact((group == lane).astype(F32), codes, (1, 0))
        code_col[...] = jnp.sum(jnp.where(key - group * CAP == lane, tall, 0.0), axis=1, keepdims=True)
        key = iota((128, KEYS), 1)
        group = twelfth(key)
        line_no = iota((128, KEYS), 0)
        flat = exact(codes, (group == line_no).astype(F32), (0, 0))
        code_row[...] = jnp.sum(jnp.where(key - group * CAP == line_no, flat, 0.0), axis=0, keepdims=True)

        def floor_of(code):
            return ((((code.astype(I32) - 1) >> 11) << 11) + 1).astype(F32)

        base_row[...] = floor_of(code_row[...])
        base_col[...] = floor_of(code_col[...])
        held = (omap[...] == r).astype(F32)
        held16 = held.astype(BF16)
        lower = (iota((64, 64), 1) < iota((64, 64), 0)).astype(F32).astype(BF16)
        ahead = (iota((128, 128), 0) < iota((128, 128), 1)).astype(F32).astype(BF16)
        spot = mm(held16, ahead, (1, 0)) + jnp.sum(mm(lower, held16, (1, 0)), axis=1, keepdims=True)
        spot = jnp.where(held > 0.0, spot, 0.0)
        for q in range(4):
            lanes = slice(q * 384, (q + 1) * 384)
            spot_row[:, lanes] = lookup(spot, (code_row[:, lanes].astype(I32) - 1) >> 11)

    def answer(p):
        return (runs.at[p], fbuf.at[my_line // 2], r1_s.at[p], r1_r.at[my_line // 2])

    mid = my_line % 2
    is_mid = c == mid

    @pl.when(active)
    def _():
        fnd[...] = jnp.full(fnd.shape, -1.0, F32)
        best_col[...] = jnp.full(best_col.shape, -1.0, F32)

        def update(q, b, both_ways):
            lanes = pl.ds(q * 384, 384)
            rows = pl.ds(b * 384, 384)
            cq, bq = code_row[:, lanes], base_row[:, lanes]
            gram = mm(keys[rows, :], keys[lanes, :], (1, 1))
            ck = code_col[rows, :]
            keep = (ck >= bq) & (ck < cq)
            fnd[q] = jnp.maximum(fnd[q], jnp.max(jnp.where(keep, gram, -1.0), axis=0, keepdims=True))
            if both_ways:
                keep = (cq >= base_col[rows, :]) & (cq < ck)
                found = jnp.max(jnp.where(keep, gram, -1.0), axis=1, keepdims=True)
                best_col[rows, :] = jnp.maximum(best_col[rows, :], found)

        for part in range(4):
            for p in range(4 * part, 4 * part + 4):
                pltpu.make_async_copy(
                    send2.at[pl.ds(0, RUN), :], keys.at[pl.ds(p * RUN, RUN), :], s2_r.at[p]
                ).wait()

            for b in range(part + 1):
                update(part, b, b < part)

        for q in range(4):
            best = fnd[q]
            if q < 3:
                diagonal = iota((128, 128), 0) == iota((128, 128), 1)
                turned = [
                    jnp.max(
                        jnp.where(diagonal, best_col[q * 384 + k * 128 : q * 384 + (k + 1) * 128, :], -2.0),
                        axis=0, keepdims=True,
                    )
                    for k in range(3)
                ]
                best = jnp.maximum(best, jnp.concatenate(turned, axis=1))
                fnd[q] = best
            for k in range(4):
                runs[q * 4 + k, :, 0:RUN] = best[:, k * RUN : (k + 1) * RUN]
        for p in reversed(range(NZ)):
            push(answer(p), at(x, (z + STEPS[p]) % NZ, mid), y, is_mid if p == 0 else False)

    for copy in pair:
        copy.wait_recv()
    bst[...] = jnp.full(bst.shape, -4.0, F32)
    own[...] = jnp.full(own.shape, -4.0, F32)

    def score(xx):
        row = iota((256, 1), 0)
        number = ((xx * NZ + (row >> 4)) * NC + c) * (NY * KB) + y * KB + (row & 15)

        def part(q, carry):
            rows = pl.ds(pl.multiple_of(q * 256, 256), 256)
            sims = mm(cbuf[xx].reshape(256, D), unit2[rows, :], (1, 1))
            bst[:, rows] = jnp.maximum(bst[:, rows], jnp.max(sims, axis=0, keepdims=True))
            here = lab2[q // 2, :, pl.ds(pl.multiple_of((q % 2) * 256, 256), 256)]
            found = jnp.max(jnp.where(number == here, sims, -4.0), axis=0, keepdims=True)
            own[:, rows] = jnp.maximum(own[:, rows], found)
            return carry

        lax.fori_loop(0, 4, part, 0)

    score(x)
    for d in range(1, 4):
        across[d - 1].wait_recv()
        score((x + NX - d) % NX)

    me_t = y * NC + c
    for q in range(8):
        rows = pl.ds((q % NC) * TOK + (q // NC) * 128, 128)
        tsnd[q, :, 0:128] = bst[:, rows]
        tsnd[q, :, 128:256] = own[:, rows]
    trcv[me_t] = tsnd[me_t]
    tops = []
    for d in range(1, 8):
        q = (me_t + d) % 8
        tops.append(remote(tsnd.at[q], trcv.at[me_t], t_s.at[d - 1], t_r.at[d - 1], at(x, z, q % NC), q // NC))
        tops[-1].start()

    for copy in pair + far + near + across + meta1 + first:
        copy.wait_send()
    for m in range(4):
        pushed(second_meta(m), at(x, target(m), core), y, to_self(m))
        pushed(second(m), at(x, target(m), core), y, to_self(m))

    for m in range(4):
        pltpu.make_async_copy(runs.at[0], fbuf.at[m], r1_r.at[m]).wait()
    for m in range(4):
        fpack[m : m + 1, :] = fbuf[m]
    mine_back = pl.ds(pl.multiple_of(mi * 8, 8), 8)
    backs = [
        remote(fpack, fall.at[mine_back, :], r2_s.at[d - 1], r2_r.at[d - 1], *slice_mate(d)) for d in range(1, 32)
    ]
    for copy in backs:
        copy.start()
    fall[mine_back, :] = fpack[...]

    @pl.when(active)
    def _():
        peaks = jnp.full((64, 1), -1.0, F32)
        for q in range(4):
            spots = spot_row[:, q * 384 : (q + 1) * 384].astype(I32)
            hit = jnp.where(iota((64, 384), 0) == spots, fnd[q], -1.0)
            peaks = jnp.maximum(peaks, jnp.max(hit, axis=1, keepdims=True))
        prow[0] = jnp.max(jnp.where(iota((64, 128), 0) == iota((64, 128), 1), peaks, -2.0), axis=0, keepdims=True)
        for d in range(1, NY):
            remote(prow.at[0], prow.at[0], p_s.at[d - 1], p_r.at[0], r, (y + d) % NY).start()

    for copy in tops:
        copy.wait_recv()
    both = jnp.max(trcv[...], axis=0)
    top_out[...] = both[:, 0:128]
    own_out[...] = both[:, 128:256]

    rows_wanted = (iota((256, 128), 0) == wanted[y, :, 0:128]).astype(F32)
    lanes_wanted = iota((128, 128), 0) == wanted[y, :, 128:256]
    for copy in backs:
        copy.wait_recv()
    picked = exact(fall[...], rows_wanted, (0, 0))
    dup_out[...] = jnp.sum(jnp.where(lanes_wanted, picked, 0.0), axis=0, keepdims=True)

    @pl.when(jnp.logical_not(active))
    def _():
        pltpu.make_async_copy(tsnd.at[0, :, 0:128], prow.at[0], p_r.at[0]).wait()

    peak_out[...] = prow[0, :, 0:64]

    for copy in tops + backs:
        copy.wait_send()

    @pl.when(active)
    def _():
        for p in range(NZ):
            pushed(answer(p), at(x, (z + STEPS[p]) % NZ, mid), y, is_mid if p == 0 else False)
        for d in range(1, NY):
            remote(prow.at[0], prow.at[0], p_s.at[d - 1], p_r.at[0], r, (y + d) % NY).wait_send()


def per_device(embeddings, centroids, labels, ranks, owner_map):
    dma = pltpu.SemaphoreType.DMA
    vmem = pltpu.VMEM
    row = jax.ShapeDtypeStruct((1, 128), F32)
    spec = pl.BlockSpec(memory_space=pltpu.VMEM)
    outs = pl.pallas_call(
        kernel,
        out_shape=(row, row, row, jax.ShapeDtypeStruct((1, 64), F32)),
        in_specs=[pl.BlockSpec(memory_space=pl.ANY)] * 5,
        out_specs=(spec,) * 4,
        scratch_shapes=[
            vmem((TOK, D), BF16),
            vmem((KB, D), F32),
            vmem((1, TOK), I32),
            vmem((1, TOK), I32),
            vmem((64, 128), I32),
            vmem((2 * TOK, D), BF16),
            vmem((2, 1, TOK), I32),
            vmem((NX, 4, 4, KB, D), BF16),
            vmem((SLOTS, D), BF16),
            vmem((SLOTS, D), BF16),
            vmem((SLOTS, D), BF16),
            vmem((KEYS, D), BF16),
            vmem((1, 1, SLOTS), F32),
            vmem((8, 1, SLOTS), F32),
            vmem((8, SLOTS), F32),
            vmem((NZ * 8, SLOTS), F32),
            vmem((KEYS, 1), F32),
            vmem((1, KEYS), F32),
            vmem((KEYS, 1), F32),
            vmem((1, KEYS), F32),
            vmem((1, KEYS), F32),
            vmem((1, 2 * TOK), F32),
            vmem((1, 2 * TOK), F32),
            vmem((8, 1, 256), F32),
            vmem((8, 1, 256), F32),
            vmem((4, 1, 384), F32),
            vmem((KEYS, 1), F32),
            vmem((NZ, 1, 128), F32),
            vmem((4, 1, 128), F32),
            vmem((8, 128), F32),
            vmem((256, 128), F32),
            vmem((NY, 1, 256), I32),
            vmem((1, 1, 128), F32),
            dma((5,)),
            dma((2,)), dma((2,)),
            dma((9,)), dma((9,)),
            dma((7,)), dma((7,)),
            dma((7,)), dma((7,)),
            dma((4,)), dma((NZ,)),
            dma((4,)), dma((NZ,)),
            dma((7,)), dma((7,)),
            dma((NZ,)), dma((4,)),
            dma((31,)), dma((31,)),
            dma((3,)), dma((1,)),
        ],
        compiler_params=pltpu.CompilerParams(
            collective_id=0, has_side_effects=True, vmem_limit_bytes=62 * 1024 * 1024
        ),
    )(
        embeddings, centroids, labels.reshape(1, TOK), ranks.reshape(1, TOK), owner_map.reshape(64, 128)
    )
    return tuple(o.reshape(-1) for o in outs)


def solution(mesh):
    placed = (P("rows", None), P(("rows", "cent"), None), P("rows"), P("rows"), P())
    return jax.shard_map(
        per_device,
        mesh=mesh,
        in_specs=placed,
        out_specs=(P(("rows", "cent")), P(("rows", "cent")), P(("rows", "cent")), P("rows")),
        check_vma=False,
    )
```

```python
import functools

import jax
import jax.numpy as jnp
from jax import lax
from jax.experimental import pallas as pl
from jax.experimental.pallas import tpu as pltpu
from jax.sharding import PartitionSpec as P

MESH = pl.DeviceIdType.MESH
F32 = jnp.float32
BF16 = jnp.bfloat16
I32 = jnp.int32

NX, NZ, NC, NY = 4, 16, 2, 4
CAP = 12
TOK = 512
D = 768
KB = 16
SLOTS = 32 * CAP
PIECE = 4 * CAP
RUN = 8 * CAP
KEYS = NZ * RUN
STEPS = [0] + [d for k in range(1, 8) for d in (k, NZ - k)] + [8]
RANKS = 2048


def iota(shape, dim):
    return lax.broadcasted_iota(I32, shape, dim)


def mm(a, b, contract, precision=None):
    return lax.dot_general(
        a, b, ((contract[:1], contract[1:]), ((), ())), precision=precision, preferred_element_type=F32
    )


def exact(a, b, contract):
    return mm(a, b, contract, lax.Precision.HIGHEST)


def unit_of(wide):
    return (wide * lax.rsqrt(jnp.sum(wide * wide, axis=-1, keepdims=True) + 1e-06)).astype(BF16)


def lookup(table, ids):
    n = ids.shape[1]
    high = (iota((64, n), 0) == (ids >> 7)).astype(F32).astype(BF16)
    picked = mm(table.astype(F32).astype(BF16), high, (0, 0))
    return jnp.sum(jnp.where(iota((128, n), 0) == (ids & 127), picked, 0.0), axis=0, keepdims=True)


def twelfth(v):
    return (v * 10923) >> 17


def nearness(dz):
    return jnp.where(dz <= 8, jnp.maximum(2 * dz - 1, 0), 2 * (NZ - dz))


def kernel(
    emb_in, cen_in, lab_in, rank_in, omap_in,
    top_out, own_out, dup_out, peak_out,
    emb, cen, lab, rank, omap,
    unit2, lab2, cbuf, send1, recv1, send2, keys, meta_s, meta_r, meta_p, meta_k, code_col, code_row, base_col, base_row, spot_row,
    bst, own, tsnd, trcv, fnd, best_col, runs, fbuf, fpack, fall, wanted, prow,
    in_s, pair_s, pair_r, a_s, a_r, s1_s, s1_r, m1_s, m1_r, s2_s, s2_r, m2_s, m2_r, t_s, t_r,
    r1_s, r1_r, r2_s, r2_r, p_s, p_r,
):
    r = lax.axis_index("rows")
    y = lax.axis_index("cent")
    c = r % NC
    z = (r // NC) % NZ
    x = r // (NC * NZ)
    me = x * NC + c

    def at(xx, zz, cc):
        return (xx * NZ + zz) * NC + cc

    def remote(src, dst, ssem, rsem, rows, cent):
        return pltpu.make_async_remote_copy(
            src_ref=src, dst_ref=dst, send_sem=ssem, recv_sem=rsem,
            device_id={"rows": rows, "cent": cent}, device_id_type=MESH,
        )

    def mate(d):
        q = (me + d) % 8
        return at(q // NC, z, q % NC)

    barrier = pltpu.get_barrier_semaphore()
    runs[...] = jnp.zeros(runs.shape, F32)
    fpack[...] = jnp.zeros(fpack.shape, F32)

    def hello(rows, cent):
        pl.semaphore_signal(barrier, inc=1, device_id={"rows": rows, "cent": cent}, device_id_type=MESH)

    mi = y * 8 + me

    def slice_mate(d):
        q = (mi + d) % 32
        return at((q % 8) // NC, z, q % NC), q // 8

    for d in range(1, 32):
        hello(*slice_mate(d))
    for d in range(1, NZ):
        for cc in range(NC):
            hello(at(x, (z + d) % NZ, cc), y)

    loads = [
        pltpu.make_async_copy(src, dst, in_s.at[k])
        for k, (src, dst) in enumerate(
            ((cen_in, cen), (lab_in, lab), (rank_in, rank), (omap_in, omap), (emb_in, emb))
        )
    ]
    for copy in loads:
        copy.start()
    for copy in loads:
        copy.wait()

    w = z % 4
    g = z // 4
    cbuf[x, g, w] = unit_of(cen[...])
    half = pl.ds(pl.multiple_of(c * TOK, TOK), TOK)
    unit2[half, :] = unit_of(emb[...].astype(F32))
    lab2[c] = lab[...]
    ids = lab[...]
    owner = lookup(omap[...], ids).astype(I32)
    named = iota((128, TOK), 0) == owner
    upper = (iota((TOK, TOK), 0) < iota((TOK, TOK), 1)).astype(F32).astype(BF16)
    before = mm(named.astype(F32).astype(BF16), upper, (1, 0))
    slot = jnp.sum(jnp.where(named, before, 0.0), axis=0, keepdims=True).astype(I32)
    xo, zo, co = owner >> 5, (owner >> 1) & 15, owner & 1
    place = zo >> 1
    mine = (co == y // 2) & (((xo + zo) & 1) == y % 2)
    line = xo * 8 + (place & 1) * 4 + (place >> 1)
    dest = jnp.where(mine, line * CAP + slot, -1)
    spread = (iota((SLOTS, TOK), 0) == dest).astype(F32)
    code = (ids * RANKS + rank[...] + 1).astype(F32)
    meta_s[0] = exact(code, spread, (1, 1))
    meta_r[me] = meta_s[0]
    send1[...] = mm(spread.astype(BF16), unit2[half, :], (1, 0)).astype(BF16)
    mine_in = pl.ds(pl.multiple_of(me * PIECE, 16), PIECE)
    recv1[mine_in, :] = send1[mine_in, :]
    plane = 2 * co + ((xo + zo) & 1)
    run_row = plane * 64 + (line >> 2) * 8 + (line & 3)
    inner = me * CAP + slot
    for q in range(NY):
        lanes = slice(q * 128, (q + 1) * 128)
        wanted[q, :, 0:128] = run_row[:, lanes]
        wanted[q, :, 128:256] = inner[:, lanes]

    pl.semaphore_wait(barrier, 31 + 2 * (NZ - 1))

    far = [
        remote(cbuf.at[x, g, w], cbuf.at[x, g, w], a_s.at[d - 1], a_r.at[d - 1], at(x, (z + 4 * d) % NZ, c), y)
        for d in range(1, 4)
    ]
    other = at(x, z, 1 - c)
    pair = [
        remote(unit2.at[half, :], unit2.at[half, :], pair_s.at[0], pair_r.at[0], other, y),
        remote(lab2.at[c], lab2.at[c], pair_s.at[1], pair_r.at[1], other, y),
    ]
    meta1 = [
        remote(meta_s.at[0], meta_r.at[me], m1_s.at[d - 1], m1_r.at[d - 1], mate(d), y) for d in range(1, 8)
    ]
    first = [
        remote(
            send1.at[pl.ds(pl.multiple_of(((me + d) % 8) * PIECE, 16), PIECE), :], recv1.at[mine_in, :],
            s1_s.at[d - 1], s1_r.at[d - 1], mate(d), y,
        )
        for d in range(1, 8)
    ]
    for copy in first + far + meta1 + pair:
        copy.start()

    for copy in far:
        copy.wait_recv()
    near = [
        remote(
            cbuf.at[x, :, w], cbuf.at[x, :, w], a_s.at[2 + d], a_r.at[2 + d], at(x, (z + dz) % NZ, c), y
        )
        for d, dz in ((1, 1), (2, NZ - 1))
    ]
    for copy in near:
        copy.start()

    parity = (x + y) % 2
    core = y // 2
    active = (c == core) & ((x + z) % 2 == y % 2)
    my_line = z // 2

    def target(m):
        return 4 * m + 2 * c + parity

    def spot_at(m):
        return nearness((z - target(m)) & 15)

    def second(m):
        place = spot_at(m)
        return (
            send2.at[pl.ds(m * RUN, RUN), :],
            keys.at[pl.ds(pl.multiple_of(place * RUN, 16), RUN), :],
            s2_s.at[m],
            s2_r.at[place],
        )

    def second_meta(m):
        place = spot_at(m)
        return (meta_p, meta_k.at[pl.ds(pl.multiple_of(place * 8, 8), 8), :], m2_s.at[m], m2_r.at[place])

    def push(parts, rows, cent, local):
        if local is False:
            remote(*parts, rows, cent).start()
            return

        @pl.when(jnp.logical_not(local))
        def _():
            remote(*parts, rows, cent).start()

        @pl.when(local)
        def _():
            pltpu.make_async_copy(parts[0], parts[1], parts[3]).start()

    def pushed(parts, rows, cent, local):
        if local is False:
            remote(*parts, rows, cent).wait_send()
            return

        @pl.when(jnp.logical_not(local))
        def _():
            remote(*parts, rows, cent).wait_send()

    def to_self(m):
        return (target(m) == z) & (c == core)

    for copy in meta1:
        copy.wait_recv()
    for j in range(8):
        meta_p[j : j + 1, :] = meta_r[j]
    for m in range(4):
        push(second_meta(m), at(x, target(m), core), y, to_self(m))

    out_row = iota((SLOTS, SLOTS), 0)
    unit_no = twelfth(out_row)
    source_row = (unit_no & 7) * PIECE + (unit_no >> 3) * CAP + (out_row - unit_no * CAP)
    order = (source_row == iota((SLOTS, SLOTS), 1)).astype(F32).astype(BF16)
    for copy in first:
        copy.wait_recv()
    send2[...] = mm(order, recv1[...], (1, 0)).astype(BF16)
    for m in range(4):
        push(second(m), at(x, target(m), core), y, to_self(m))

    for copy in near:
        copy.wait_recv()
    up, down = (w + 3) % 4, (w + 1) % 4
    passed = [
        remote(
            cbuf.at[x, 0:2, down], cbuf.at[x, 0:2, down], a_s.at[5], a_r.at[5], at(x, (z + NZ - 1) % NZ, c), y
        ),
        remote(cbuf.at[x, 2:4, up], cbuf.at[x, 2:4, up], a_s.at[9], a_r.at[9], at(x, (z + 1) % NZ, c), y),
    ]
    for copy in passed:
        copy.start()
    for copy in passed:
        copy.wait_recv()
    across = [
        remote(cbuf.at[x], cbuf.at[x], a_s.at[5 + d], a_r.at[5 + d], at((x + d) % NX, z, c), y) for d in range(1, 4)
    ]
    for copy in across:
        copy.start()

    @pl.when(active)
    def _():
        for zz in range(NZ):
            pltpu.make_async_copy(meta_p, meta_k.at[pl.ds(zz * 8, 8), :], m2_r.at[zz]).wait()
        offset = (x * NC + my_line % 2) * PIECE + (my_line // 2) * CAP
        pick = ((iota((SLOTS, 128), 0) == iota((SLOTS, 128), 1) + offset) & (iota((SLOTS, 128), 1) < CAP)).astype(F32)
        codes = exact(meta_k[...], pick, (1, 0))
        key = iota((KEYS, 128), 0)
        group = twelfth(key)
        lane = iota((KEYS, 128), 1)
        tall = exact((group == lane).astype(F32), codes, (1, 0))
        code_col[...] = jnp.sum(jnp.where(key - group * CAP == lane, tall, 0.0), axis=1, keepdims=True)
        key = iota((128, KEYS), 1)
        group = twelfth(key)
        line_no = iota((128, KEYS), 0)
        flat = exact(codes, (group == line_no).astype(F32), (0, 0))
        code_row[...] = jnp.sum(jnp.where(key - group * CAP == line_no, flat, 0.0), axis=0, keepdims=True)

        def floor_of(code):
            return ((((code.astype(I32) - 1) >> 11) << 11) + 1).astype(F32)

        base_row[...] = floor_of(code_row[...])
        base_col[...] = floor_of(code_col[...])
        held = (omap[...] == r).astype(F32)
        held16 = held.astype(BF16)
        lower = (iota((64, 64), 1) < iota((64, 64), 0)).astype(F32).astype(BF16)
        ahead = (iota((128, 128), 0) < iota((128, 128), 1)).astype(F32).astype(BF16)
        spot = mm(held16, ahead, (1, 0)) + jnp.sum(mm(lower, held16, (1, 0)), axis=1, keepdims=True)
        spot = jnp.where(held > 0.0, spot, 0.0)
        for q in range(4):
            lanes = slice(q * 384, (q + 1) * 384)
            spot_row[:, lanes] = lookup(spot, (code_row[:, lanes].astype(I32) - 1) >> 11)

    def answer(p):
        return (runs.at[p], fbuf.at[my_line // 2], r1_s.at[p], r1_r.at[my_line // 2])

    mid = my_line % 2
    is_mid = c == mid

    @pl.when(active)
    def _():
        fnd[...] = jnp.full(fnd.shape, -1.0, F32)
        best_col[...] = jnp.full(best_col.shape, -1.0, F32)

        def update(q, b, both_ways):
            lanes = pl.ds(q * 384, 384)
            rows = pl.ds(b * 384, 384)
            cq, bq = code_row[:, lanes], base_row[:, lanes]
            gram = mm(keys[rows, :], keys[lanes, :], (1, 1))
            ck = code_col[rows, :]
            keep = (ck >= bq) & (ck < cq)
            fnd[q] = jnp.maximum(fnd[q], jnp.max(jnp.where(keep, gram, -1.0), axis=0, keepdims=True))
            if both_ways:
                keep = (cq >= base_col[rows, :]) & (cq < ck)
                found = jnp.max(jnp.where(keep, gram, -1.0), axis=1, keepdims=True)
                best_col[rows, :] = jnp.maximum(best_col[rows, :], found)

        for part in range(4):
            for p in range(4 * part, 4 * part + 4):
                pltpu.make_async_copy(
                    send2.at[pl.ds(0, RUN), :], keys.at[pl.ds(p * RUN, RUN), :], s2_r.at[p]
                ).wait()

            for b in range(part + 1):
                update(part, b, b < part)

        for q in range(4):
            best = fnd[q]
            if q < 3:
                diagonal = iota((128, 128), 0) == iota((128, 128), 1)
                turned = [
                    jnp.max(
                        jnp.where(diagonal, best_col[q * 384 + k * 128 : q * 384 + (k + 1) * 128, :], -2.0),
                        axis=0, keepdims=True,
                    )
                    for k in range(3)
                ]
                best = jnp.maximum(best, jnp.concatenate(turned, axis=1))
                fnd[q] = best
            for k in range(4):
                runs[q * 4 + k, :, 0:RUN] = best[:, k * RUN : (k + 1) * RUN]
        for p in reversed(range(NZ)):
            push(answer(p), at(x, (z + STEPS[p]) % NZ, mid), y, is_mid if p == 0 else False)

    for copy in pair:
        copy.wait_recv()
    bst[...] = jnp.full(bst.shape, -4.0, F32)
    own[...] = jnp.full(own.shape, -4.0, F32)

    def score(xx):
        row = iota((256, 1), 0)
        number = ((xx * NZ + (row >> 4)) * NC + c) * (NY * KB) + y * KB + (row & 15)

        def part(q, carry):
            rows = pl.ds(pl.multiple_of(q * 256, 256), 256)
            sims = mm(cbuf[xx].reshape(256, D), unit2[rows, :], (1, 1))
            bst[:, rows] = jnp.maximum(bst[:, rows], jnp.max(sims, axis=0, keepdims=True))
            here = lab2[q // 2, :, pl.ds(pl.multiple_of((q % 2) * 256, 256), 256)]
            found = jnp.max(jnp.where(number == here, sims, -4.0), axis=0, keepdims=True)
            own[:, rows] = jnp.maximum(own[:, rows], found)
            return carry

        lax.fori_loop(0, 4, part, 0)

    score(x)
    for d in range(1, 4):
        across[d - 1].wait_recv()
        score((x + NX - d) % NX)

    me_t = y * NC + c
    for q in range(8):
        rows = pl.ds((q % NC) * TOK + (q // NC) * 128, 128)
        tsnd[q, :, 0:128] = bst[:, rows]
        tsnd[q, :, 128:256] = own[:, rows]
    trcv[me_t] = tsnd[me_t]
    tops = []
    for d in range(1, 8):
        q = (me_t + d) % 8
        tops.append(remote(tsnd.at[q], trcv.at[me_t], t_s.at[d - 1], t_r.at[d - 1], at(x, z, q % NC), q // NC))
        tops[-1].start()

    for copy in pair + far + near + passed + across + meta1 + first:
        copy.wait_send()
    for m in range(4):
        pushed(second_meta(m), at(x, target(m), core), y, to_self(m))
        pushed(second(m), at(x, target(m), core), y, to_self(m))

    for m in range(4):
        pltpu.make_async_copy(runs.at[0], fbuf.at[m], r1_r.at[m]).wait()
    for m in range(4):
        fpack[m : m + 1, :] = fbuf[m]
    mine_back = pl.ds(pl.multiple_of(mi * 8, 8), 8)
    backs = [
        remote(fpack, fall.at[mine_back, :], r2_s.at[d - 1], r2_r.at[d - 1], *slice_mate(d)) for d in range(1, 32)
    ]
    for copy in backs:
        copy.start()
    fall[mine_back, :] = fpack[...]

    @pl.when(active)
    def _():
        peaks = jnp.full((64, 1), -1.0, F32)
        for q in range(4):
            spots = spot_row[:, q * 384 : (q + 1) * 384].astype(I32)
            hit = jnp.where(iota((64, 384), 0) == spots, fnd[q], -1.0)
            peaks = jnp.maximum(peaks, jnp.max(hit, axis=1, keepdims=True))
        prow[0] = jnp.max(jnp.where(iota((64, 128), 0) == iota((64, 128), 1), peaks, -2.0), axis=0, keepdims=True)
        for d in range(1, NY):
            remote(prow.at[0], prow.at[0], p_s.at[d - 1], p_r.at[0], r, (y + d) % NY).start()

    for copy in tops:
        copy.wait_recv()
    both = jnp.max(trcv[...], axis=0)
    top_out[...] = both[:, 0:128]
    own_out[...] = both[:, 128:256]

    rows_wanted = (iota((256, 128), 0) == wanted[y, :, 0:128]).astype(F32)
    lanes_wanted = iota((128, 128), 0) == wanted[y, :, 128:256]
    for copy in backs:
        copy.wait_recv()
    picked = exact(fall[...], rows_wanted, (0, 0))
    dup_out[...] = jnp.sum(jnp.where(lanes_wanted, picked, 0.0), axis=0, keepdims=True)

    @pl.when(jnp.logical_not(active))
    def _():
        pltpu.make_async_copy(tsnd.at[0, :, 0:128], prow.at[0], p_r.at[0]).wait()

    peak_out[...] = prow[0, :, 0:64]

    for copy in tops + backs:
        copy.wait_send()

    @pl.when(active)
    def _():
        for p in range(NZ):
            pushed(answer(p), at(x, (z + STEPS[p]) % NZ, mid), y, is_mid if p == 0 else False)
        for d in range(1, NY):
            remote(prow.at[0], prow.at[0], p_s.at[d - 1], p_r.at[0], r, (y + d) % NY).wait_send()


def per_device(embeddings, centroids, labels, ranks, owner_map):
    dma = pltpu.SemaphoreType.DMA
    vmem = pltpu.VMEM
    row = jax.ShapeDtypeStruct((1, 128), F32)
    spec = pl.BlockSpec(memory_space=pltpu.VMEM)
    outs = pl.pallas_call(
        kernel,
        out_shape=(row, row, row, jax.ShapeDtypeStruct((1, 64), F32)),
        in_specs=[pl.BlockSpec(memory_space=pl.ANY)] * 5,
        out_specs=(spec,) * 4,
        scratch_shapes=[
            vmem((TOK, D), BF16),
            vmem((KB, D), F32),
            vmem((1, TOK), I32),
            vmem((1, TOK), I32),
            vmem((64, 128), I32),
            vmem((2 * TOK, D), BF16),
            vmem((2, 1, TOK), I32),
            vmem((NX, 4, 4, KB, D), BF16),
            vmem((SLOTS, D), BF16),
            vmem((SLOTS, D), BF16),
            vmem((SLOTS, D), BF16),
            vmem((KEYS, D), BF16),
            vmem((1, 1, SLOTS), F32),
            vmem((8, 1, SLOTS), F32),
            vmem((8, SLOTS), F32),
            vmem((NZ * 8, SLOTS), F32),
            vmem((KEYS, 1), F32),
            vmem((1, KEYS), F32),
            vmem((KEYS, 1), F32),
            vmem((1, KEYS), F32),
            vmem((1, KEYS), F32),
            vmem((1, 2 * TOK), F32),
            vmem((1, 2 * TOK), F32),
            vmem((8, 1, 256), F32),
            vmem((8, 1, 256), F32),
            vmem((4, 1, 384), F32),
            vmem((KEYS, 1), F32),
            vmem((NZ, 1, 128), F32),
            vmem((4, 1, 128), F32),
            vmem((8, 128), F32),
            vmem((256, 128), F32),
            vmem((NY, 1, 256), I32),
            vmem((1, 1, 128), F32),
            dma((5,)),
            dma((2,)), dma((2,)),
            dma((10,)), dma((10,)),
            dma((7,)), dma((7,)),
            dma((7,)), dma((7,)),
            dma((4,)), dma((NZ,)),
            dma((4,)), dma((NZ,)),
            dma((7,)), dma((7,)),
            dma((NZ,)), dma((4,)),
            dma((31,)), dma((31,)),
            dma((3,)), dma((1,)),
        ],
        compiler_params=pltpu.CompilerParams(
            collective_id=0, has_side_effects=True, vmem_limit_bytes=62 * 1024 * 1024
        ),
    )(
        embeddings, centroids, labels.reshape(1, TOK), ranks.reshape(1, TOK), owner_map.reshape(64, 128)
    )
    return tuple(o.reshape(-1) for o in outs)


def solution(mesh):
    placed = (P("rows", None), P(("rows", "cent"), None), P("rows"), P("rows"), P())
    return jax.shard_map(
        per_device,
        mesh=mesh,
        in_specs=placed,
        out_specs=(P(("rows", "cent")), P(("rows", "cent")), P(("rows", "cent")), P("rows")),
        check_vma=False,
    )
```
